32 devices in a mesh: kv: 4 (over y, core), blk: 8 (over z, x).
Axes of the slice: x: 2, y: 2, z: 4, core: 2. Of those that a mesh axis runs over, the one named last changes fastest.
Arguments:
- queries: bfloat16 [256, 8192], P('blk', 'kv'), may hold values from -40 to 40
- draft_token_keys: bfloat16 [256, 1024], P('blk', 'kv'), may hold values from -15 to 15
- draft_token_values: bfloat16 [256, 1024], P('blk', 'kv'), may hold values from -6 to 6
- cached_key_vectors: bfloat16 [4, 4096, 1024], P(None, 'blk', 'kv'), may hold values from -40 to 40
- cached_value_vectors: bfloat16 [4, 4096, 1024], P(None, 'blk', 'kv'), may hold values from -6 to 6
- out_weight: bfloat16 [8192, 8192], P('kv', 'blk'), may hold values from -0.5 to 0.5
- lengths: int32 [4], replicated, may hold values from 256 to 4088, as said below
- parents: int32 [4, 64], replicated, may hold values from 0 to 62, as said below
- accepted_nodes: int32 [4, 8], replicated, may hold values from 0 to 62, as said below
- accepted_count: int32 [4], replicated, may hold values from 1 to 8, as said below
Outputs:
- projected: bfloat16 [256, 8192], P('kv', 'blk')
- new_cache_keys: bfloat16 [4, 4096, 1024], P(None, 'blk', 'kv')
- new_cache_values: bfloat16 [4, 4096, 1024], P(None, 'blk', 'kv')
The draws below stay inside these ranges and needn't reach their ends.
Inputs may be any that keep to these rules, and one draw needn't show every extreme that they name: `lengths`: some request has exactly 4088, some exactly 256. parents[r, 0] = 0 and parents[r, i] < i for i >= 1. accepted_nodes[r, 0] = 0 and accepted_nodes[r, k] is a child of accepted_nodes[r, k - 1] in request r's tree; only the first accepted_count[r] entries are used. `accepted_count`: some request has exactly 8, some exactly 1.
All inputs are finite; a program needn't handle non-finite values.
Results may differ from the reference program's by a relative error of at most 0.0055.
Values may be sent and summed in bfloat16 or wider, within the bound.
A program may use at most 64 MiB of HBM per device.

```python
import math
import jax
import jax.numpy as jnp
from jax import lax

D = 8192
QUERY_HEADS = 64
KEY_VALUE_HEADS = 8
HEAD_SIZE = 128
TREE_TOKENS = 64
ACC = 8
CONTEXT_LENGTH = 4096
REQUEST_COUNT = 4
DRAFT_TOKENS = 256
BLOCK_POSITIONS = 512
N_BLK = 8


def draw_queries(key, part):
    inner_product = jax.random.fold_in(key, 11)
    attention_output = jnp.clip(jax.random.normal(inner_product, (DRAFT_TOKENS, QUERY_HEADS * HEAD_SIZE), jnp.float32), -6.0, 6.0)
    return attention_output.astype(jnp.bfloat16)


def draw_cached_key_vectors(key, part):
    inner_product = jax.random.fold_in(key, 13)
    attention_output = jnp.clip(jax.random.normal(inner_product, (REQUEST_COUNT, CONTEXT_LENGTH, KEY_VALUE_HEADS * HEAD_SIZE), jnp.float32), -6.0, 6.0)
    return attention_output.astype(jnp.bfloat16)


def pinned_ends(key, salt, lowest, highest):
    values = jax.random.randint(jax.random.fold_in(key, salt), (REQUEST_COUNT,), lowest, highest + 1)
    chosen = jax.random.permutation(jax.random.fold_in(key, salt + 1), REQUEST_COUNT)
    values = jnp.where(jnp.arange(REQUEST_COUNT) == chosen[0], highest, values)
    values = jnp.where(jnp.arange(REQUEST_COUNT) == chosen[1], lowest, values)
    return values.astype(jnp.int32)


def draw_lengths(key, part):
    return pinned_ends(key, 41, CONTEXT_LENGTH // 16, CONTEXT_LENGTH - ACC)


def draw_accepted_count(key, part):
    return pinned_ends(key, 47, 1, ACC)


def tree_draw(key):
    inner_product = jax.random.fold_in(key, 53)
    choices_base = jnp.broadcast_to(jnp.arange(1, TREE_TOKENS - 2, dtype=jnp.int32)[None, :], (REQUEST_COUNT, TREE_TOKENS - 3))
    shuffled = jax.random.permutation(jax.random.fold_in(inner_product, 1), choices_base, axis=1, independent=True)
    chosen = jnp.sort(shuffled[:, :ACC - 2], axis=1)
    path_nodes = jnp.concatenate([jnp.zeros((REQUEST_COUNT, 1), jnp.int32), chosen, jnp.full((REQUEST_COUNT, 1), TREE_TOKENS - 2, jnp.int32)], axis=1)
    upper = jnp.maximum(jnp.arange(TREE_TOKENS, dtype=jnp.int32), 1)
    parent_rows = jax.random.randint(jax.random.fold_in(inner_product, 3), (REQUEST_COUNT, TREE_TOKENS), 0, upper[None, :])
    parent_rows = parent_rows.at[:, TREE_TOKENS - 1].set(TREE_TOKENS - 2)
    request_rows = jnp.broadcast_to(jnp.arange(REQUEST_COUNT, dtype=jnp.int32)[:, None], (REQUEST_COUNT, ACC - 1))
    parent_rows = parent_rows.at[request_rows, path_nodes[:, 1:]].set(path_nodes[:, :-1])
    return (parent_rows.astype(jnp.int32), path_nodes.astype(jnp.int32))


def draw_parents(key, part):
    return tree_draw(key)[0]


def draw_accepted_nodes(key, part):
    return tree_draw(key)[1]


def block_levels(own_key, shape, cuts, least, high):
    gain, own = 1.0, jax.random.fold_in(own_key, 6)
    for axis_at, parts in cuts:
        draws = jnp.exp(jax.random.uniform(jax.random.fold_in(own, axis_at), (parts,), jnp.float32, least / len(cuts), high / len(cuts)))
        gain = gain * jnp.repeat(draws, shape[axis_at] // parts).reshape([-1 if axis == axis_at else 1 for axis in range(len(shape))])
    return gain


def normal_values(key, shape, width, bound, shards=(), held_as=jnp.bfloat16):
    loudness = block_levels(key, shape, shards, -0.22, 0.18) if shards else 1.0
    entries = jax.random.normal(key, shape, jnp.float32) * width * loudness
    return jnp.minimum(jnp.maximum(entries, -bound), bound).astype(held_as)


def setup_inputs(seed: int = 0) -> dict:
    seeds = jax.random.split(jax.random.key(seed), 11)
    queries = draw_queries(jax.random.fold_in(seeds[10], 71), 0)
    draft_token_keys = normal_values(seeds[1], (DRAFT_TOKENS, KEY_VALUE_HEADS * HEAD_SIZE), 3.0, 15.0, ((0, 8), (1, 4)))
    draft_token_values = normal_values(seeds[2], (DRAFT_TOKENS, KEY_VALUE_HEADS * HEAD_SIZE), 1.0, 6.0, ((0, 8), (1, 4)))
    cached_key_vectors = draw_cached_key_vectors(jax.random.fold_in(seeds[10], 71), 0)
    cached_value_vectors = normal_values(seeds[4], (REQUEST_COUNT, CONTEXT_LENGTH, KEY_VALUE_HEADS * HEAD_SIZE), 1.0, 6.0, ((1, 8), (2, 4)))
    out_weight = normal_values(seeds[5], (QUERY_HEADS * HEAD_SIZE, D), (QUERY_HEADS * HEAD_SIZE // 64) ** -0.5, 0.5, ((0, 4), (1, 8)))
    lengths = draw_lengths(jax.random.fold_in(seeds[10], 71), 0)
    parents = draw_parents(jax.random.fold_in(seeds[10], 71), 0)
    accepted_nodes = draw_accepted_nodes(jax.random.fold_in(seeds[10], 71), 0)
    accepted_count = draw_accepted_count(jax.random.fold_in(seeds[10], 71), 0)
    return {"queries": queries, "draft_token_keys": draft_token_keys, "draft_token_values": draft_token_values, "cached_key_vectors": cached_key_vectors, "cached_value_vectors": cached_value_vectors, "out_weight": out_weight, "lengths": lengths, "parents": parents, "accepted_nodes": accepted_nodes, "accepted_count": accepted_count}


NEG_FLOOR = -1e+30

def ancestors(parent_rows):
    node_ids = jnp.arange(TREE_TOKENS, dtype=jnp.int32)
    parent_link = ((parent_rows[:, :, None] == node_ids[None, None, :]) & (node_ids[None, :, None] >= 1)).astype(jnp.float32)
    reachable = jnp.eye(TREE_TOKENS, dtype=jnp.float32)[None] + parent_link
    for doubling in range((TREE_TOKENS - 1).bit_length()):
        reachable = jnp.minimum(reachable + jnp.einsum('rij,rjk->rik', reachable, reachable, precision=lax.Precision.HIGHEST), 1.0)
    return reachable

def partial_softmax(query_vectors, key_rows, value_rows, usable, score_scale):
    scores = jnp.einsum('rtkgh,rbpkh->brkgtp', query_vectors.astype(jnp.float32), key_rows.astype(jnp.float32)) * score_scale
    scores = jnp.where(usable, scores, NEG_FLOOR)
    peak_score = lax.optimization_barrier(jnp.max(scores, axis=-1))
    weights = jnp.where(usable, jnp.exp(scores - peak_score[..., None]), 0.0)
    weight_sum = lax.optimization_barrier(jnp.sum(weights, axis=-1))
    rounded = lax.optimization_barrier(weights.astype(jnp.bfloat16))
    weighted = jnp.einsum('brkgtp,rbpkh->brtkgh', rounded.astype(jnp.float32), value_rows.astype(jnp.float32))
    block_count, req_count, kv_count, query_group_width, row_count = peak_score.shape
    weighted = weighted.reshape(block_count, req_count * row_count, kv_count * query_group_width * value_rows.shape[-1])
    peak_score = peak_score.transpose(0, 1, 4, 2, 3).reshape(block_count, req_count * row_count, kv_count * query_group_width)
    weight_sum = weight_sum.transpose(0, 1, 4, 2, 3).reshape(block_count, req_count * row_count, kv_count * query_group_width)
    return (weighted, peak_score, weight_sum)

def merge_parts(cache_part, draft_part, head_dim):
    cache_out, cache_peak, cache_sum = cache_part
    draft_out, draft_peak, draft_sum = draft_part
    cache_out = cache_out.astype(jnp.float32)
    overall = jnp.maximum(lax.optimization_barrier(jnp.max(cache_peak, axis=0)), draft_peak[0])
    cache_factor = jnp.exp(cache_peak - overall[None])
    draft_factor = jnp.exp(draft_peak[0] - overall)
    denominator = lax.optimization_barrier(jnp.sum(cache_factor * cache_sum, axis=0)) + draft_factor * draft_sum[0]
    block_count, row_count, head_count = cache_peak.shape
    numerator = lax.optimization_barrier(jnp.sum(cache_factor[..., None] * cache_out.reshape(block_count, row_count, head_count, head_dim), axis=0))
    numerator = numerator + draft_factor[..., None] * draft_out[0].reshape(row_count, head_count, head_dim)
    return (numerator / denominator[..., None]).reshape(row_count, head_count * head_dim).astype(jnp.bfloat16)

def reference(queries, draft_token_keys, draft_token_values, cached_key_vectors, cached_value_vectors, out_weight, lengths, parents, accepted_nodes, accepted_count):
    query_group_width = QUERY_HEADS // KEY_VALUE_HEADS
    score_scale = 1.0 / math.sqrt(HEAD_SIZE)
    positions = jnp.arange(CONTEXT_LENGTH, dtype=jnp.int32).reshape(N_BLK, 1, 1, 1, 1, BLOCK_POSITIONS)

    def one_request(request_number):
        leading_row = request_number * TREE_TOKENS
        query_vectors = lax.dynamic_slice_in_dim(queries, leading_row, TREE_TOKENS, 0).reshape(1, TREE_TOKENS, KEY_VALUE_HEADS, query_group_width, HEAD_SIZE)
        request_tree_keys = lax.dynamic_slice_in_dim(draft_token_keys, leading_row, TREE_TOKENS, 0).reshape(1, 1, TREE_TOKENS, KEY_VALUE_HEADS, HEAD_SIZE)
        request_tree_values = lax.dynamic_slice_in_dim(draft_token_values, leading_row, TREE_TOKENS, 0).reshape(1, 1, TREE_TOKENS, KEY_VALUE_HEADS, HEAD_SIZE)
        keys_of_block = lax.dynamic_index_in_dim(cached_key_vectors, request_number, 0, False).reshape(1, N_BLK, BLOCK_POSITIONS, KEY_VALUE_HEADS, HEAD_SIZE)
        values_of_block = lax.dynamic_index_in_dim(cached_value_vectors, request_number, 0, False).reshape(1, N_BLK, BLOCK_POSITIONS, KEY_VALUE_HEADS, HEAD_SIZE)
        length = lax.dynamic_index_in_dim(lengths, request_number, 0, False)
        parent_rows = lax.dynamic_slice_in_dim(parents, request_number, 1, 0)
        reachable = ancestors(parent_rows)
        cache_out, cache_peak, cache_sum = partial_softmax(query_vectors, keys_of_block, values_of_block, positions < length, score_scale)
        cache_out = lax.optimization_barrier(cache_out.astype(jnp.bfloat16))
        draft_usable = (reachable > 0.5)[None, :, None, None, :, :]
        draft_part = partial_softmax(query_vectors, request_tree_keys, request_tree_values, draft_usable, score_scale)
        return merge_parts((cache_out, cache_peak, cache_sum), draft_part, HEAD_SIZE)
    attention = lax.map(one_request, jnp.arange(REQUEST_COUNT, dtype=jnp.int32)).reshape(DRAFT_TOKENS, QUERY_HEADS * HEAD_SIZE)
    projected = jnp.dot(attention, out_weight, preferred_element_type=jnp.float32).astype(jnp.bfloat16)
    offset = jnp.arange(CONTEXT_LENGTH, dtype=jnp.int32)[None, :] - lengths[:, None]
    written = (offset >= 0) & (offset < accepted_count[:, None])
    slot_index = jnp.clip(offset, 0, ACC - 1).astype(jnp.int32)
    node_ids = jnp.take_along_axis(accepted_nodes, slot_index, axis=1)
    source_rows = (jnp.arange(REQUEST_COUNT, dtype=jnp.int32)[:, None] * TREE_TOKENS + node_ids).astype(jnp.int32)
    new_cache_keys = jnp.where(written[:, :, None], draft_token_keys[source_rows], cached_key_vectors)
    new_cache_values = jnp.where(written[:, :, None], draft_token_values[source_rows], cached_value_vectors)
    return (projected, new_cache_keys, new_cache_values)
```

```python
import functools
import math

import jax
import jax.numpy as jnp
from jax import lax
from jax.experimental import pallas as pl
from jax.experimental.pallas import tpu as pltpu
from jax.sharding import PartitionSpec as P

HEAD_SIZE = 128
TREE_TOKENS = 64
ACC = 8


NEG_FLOOR = -1e30


def ancestors(parent_rows):
    node_ids = jnp.arange(TREE_TOKENS, dtype=jnp.int32)
    parent_link = (
        (parent_rows[:, :, None] == node_ids[None, None, :]) & (node_ids[None, :, None] >= 1)
    ).astype(jnp.float32)
    reachable = jnp.eye(TREE_TOKENS, dtype=jnp.float32)[None] + parent_link
    for doubling in range((TREE_TOKENS - 1).bit_length()):
        reachable = jnp.minimum(
            reachable
            + jnp.einsum("rij,rjk->rik", reachable, reachable, precision=lax.Precision.HIGHEST),
            1.0,
        )
    return reachable


def partial_softmax(query_vectors, key_rows, value_rows, usable, score_scale):
    scores = (
        jnp.einsum(
            "rtkgh,rbpkh->brkgtp", query_vectors, key_rows, preferred_element_type=jnp.float32
        )
        * score_scale
    )
    scores = jnp.where(usable, scores, NEG_FLOOR)
    peak_score = jnp.max(scores, axis=-1)
    weights = jnp.where(usable, jnp.exp(scores - peak_score[..., None]), 0.0)
    weight_sum = jnp.sum(weights, axis=-1)
    weighted = jnp.einsum(
        "brkgtp,rbpkh->brtkgh",
        weights.astype(jnp.bfloat16),
        value_rows,
        preferred_element_type=jnp.float32,
    )
    block_count, req_count, kv_count, query_group_width, row_count = peak_score.shape
    weighted = weighted.reshape(
        block_count, req_count * row_count, kv_count * query_group_width * value_rows.shape[-1]
    )
    peak_score = peak_score.transpose(0, 1, 4, 2, 3).reshape(
        block_count, req_count * row_count, kv_count * query_group_width
    )
    weight_sum = weight_sum.transpose(0, 1, 4, 2, 3).reshape(
        block_count, req_count * row_count, kv_count * query_group_width
    )
    return (weighted, peak_score, weight_sum)


def merge_parts(cache_part, draft_part, head_dim):
    cache_out, cache_peak, cache_sum = cache_part
    draft_out, draft_peak, draft_sum = draft_part
    cache_out = cache_out.astype(jnp.float32)
    overall = jnp.maximum(jnp.max(cache_peak, axis=0), draft_peak[0])
    cache_factor = jnp.exp(cache_peak - overall[None])
    draft_factor = jnp.exp(draft_peak[0] - overall)
    denominator = jnp.sum(cache_factor * cache_sum, axis=0) + draft_factor * draft_sum[0]
    block_count, row_count, head_count = cache_peak.shape
    numerator = jnp.sum(
        cache_factor[..., None] * cache_out.reshape(block_count, row_count, head_count, head_dim),
        axis=0,
    )
    numerator = numerator + draft_factor[..., None] * draft_out[0].reshape(
        row_count, head_count, head_dim
    )
    return (
        (numerator / denominator[..., None])
        .reshape(row_count, head_count * head_dim)
        .astype(jnp.bfloat16)
    )


def place_rows(sources, slot_index, written, cache_rows):
    slot_ids = jnp.arange(sources.shape[1], dtype=jnp.int32)
    selector = ((slot_index[:, :, None] == slot_ids[None, None, :]) & written[:, :, None]).astype(
        jnp.bfloat16
    )
    placed = jnp.einsum(
        "rps,rsc->rpc", selector, sources, preferred_element_type=jnp.float32
    ).astype(jnp.bfloat16)
    return jnp.where(written[:, :, None], placed, cache_rows)


def on_device(
    queries,
    draft_token_keys,
    draft_token_values,
    cached_key_vectors,
    cached_value_vectors,
    out_weight,
    lengths,
    parents,
    accepted_nodes,
    accepted_count,
):
    block_count = lax.axis_size("blk")
    my_block = lax.axis_index("blk")
    rows_dev, width_q = queries.shape
    requests = lengths.shape[0]
    cache_width = cached_key_vectors.shape[2]
    kv_local = cache_width // HEAD_SIZE
    query_group_width = width_q // (kv_local * HEAD_SIZE)
    block_len = cached_key_vectors.shape[1]
    score_scale = 1.0 / math.sqrt(HEAD_SIZE)
    leading_row = my_block * rows_dev
    my_request = leading_row // TREE_TOKENS
    node_start = leading_row - my_request * TREE_TOKENS
    local_queries = queries.reshape(1, rows_dev, kv_local, query_group_width, HEAD_SIZE)
    gathered_keys, gathered_values = (
        lax.all_gather(draft_token_keys, "blk", axis=0, tiled=True),
        lax.all_gather(draft_token_values, "blk", axis=0, tiled=True),
    )
    tree_keys = lax.dynamic_slice_in_dim(
        gathered_keys, my_request * TREE_TOKENS, TREE_TOKENS, 0
    ).reshape(1, 1, TREE_TOKENS, kv_local, HEAD_SIZE)
    tree_values = lax.dynamic_slice_in_dim(
        gathered_values, my_request * TREE_TOKENS, TREE_TOKENS, 0
    ).reshape(1, 1, TREE_TOKENS, kv_local, HEAD_SIZE)
    reachable = ancestors(lax.dynamic_slice_in_dim(parents, my_request, 1, 0))
    own_reach = lax.dynamic_slice_in_dim(reachable, node_start, rows_dev, 1)
    draft_usable = (own_reach > 0.5)[None, :, None, None, :, :]
    draft_part = partial_softmax(local_queries, tree_keys, tree_values, draft_usable, score_scale)
    every_query = lax.all_gather(queries, "blk", axis=0, tiled=True)
    all_queries = every_query.reshape(requests, TREE_TOKENS, kv_local, query_group_width, HEAD_SIZE)
    positions = my_block * block_len + jnp.arange(block_len, dtype=jnp.int32)
    usable = (positions[None, :] < lengths[:, None])[None, :, None, None, None, :]
    local_out, local_peak, local_sum = partial_softmax(
        all_queries,
        cached_key_vectors.reshape(requests, 1, block_len, kv_local, HEAD_SIZE),
        cached_value_vectors.reshape(requests, 1, block_len, kv_local, HEAD_SIZE),
        usable,
        score_scale,
    )
    moved_out = lax.all_to_all(
        local_out[0].astype(jnp.bfloat16), "blk", split_axis=0, concat_axis=0, tiled=True
    )
    moved_peak, moved_sum = (
        lax.all_to_all(local_peak[0], "blk", split_axis=0, concat_axis=0, tiled=True),
        lax.all_to_all(local_sum[0], "blk", split_axis=0, concat_axis=0, tiled=True),
    )
    cache_part = (
        moved_out.reshape(block_count, rows_dev, -1),
        moved_peak.reshape(block_count, rows_dev, -1),
        moved_sum.reshape(block_count, rows_dev, -1),
    )
    attention = merge_parts(cache_part, draft_part, HEAD_SIZE)
    every_row = lax.all_gather(attention, "blk", axis=0, tiled=True)
    projected = lax.psum_scatter(
        jnp.dot(every_row, out_weight, preferred_element_type=jnp.float32),
        "kv",
        scatter_dimension=0,
        tiled=True,
    ).astype(jnp.bfloat16)
    positions_here = my_block * block_len + jnp.arange(block_len, dtype=jnp.int32)
    offset = positions_here[None, :] - lengths[:, None]
    written = (offset >= 0) & (offset < accepted_count[:, None])
    slot_match = offset[:, :, None] == jnp.arange(ACC, dtype=jnp.int32)[None, None, :]
    node_ids = jnp.sum(jnp.where(slot_match, accepted_nodes[:, None, :], 0), axis=-1)
    new_cache_keys = place_rows(
        gathered_keys.reshape(requests, TREE_TOKENS, cache_width),
        node_ids,
        written,
        cached_key_vectors,
    )
    new_cache_values = place_rows(
        gathered_values.reshape(requests, TREE_TOKENS, cache_width),
        node_ids,
        written,
        cached_value_vectors,
    )
    return (projected, new_cache_keys, new_cache_values)


LOG2E = 1.4426950408889634
MESH_ID = pl.DeviceIdType.MESH
ABSENT = -1e20


def fused_kernel(
    z_count,
    kv_count,
    len_ref,
    count_ref,
    nodes_ref,
    parents_ref,
    q_ref,
    dk_ref,
    dv_ref,
    key_hbm,
    value_hbm,
    weight_hbm,
    out_ref,
    new_key_hbm,
    new_value_hbm,
    gq,
    keys,
    values,
    weight,
    own_o,
    own_st,
    xs_o,
    xs_st,
    xr_o,
    xr_st,
    zs_o,
    zs_st,
    zr_o,
    zr_st,
    ag,
    rs_send,
    rs_recv,
    local_sem,
    gz_send,
    gz_recv,
    gx_send,
    gx_recv,
    x_send,
    x_recv,
    z_send,
    z_recv,
    az_send,
    az_recv,
    ax_send,
    ax_recv,
    r_send,
    r_recv,
):
    kv = lax.axis_index("kv")
    blk = lax.axis_index("blk")
    z = blk // 2
    x = blk % 2
    other = 1 - x
    partner = (kv, z * 2 + other)
    rows, width_q = q_ref.shape
    width_kv = dk_ref.shape[1]
    groups = width_kv // HEAD_SIZE
    heads = width_q // width_kv
    cols = rows * heads
    requests, block_len, _ = keys.shape
    scale = LOG2E / math.sqrt(HEAD_SIZE)

    def z_at(step):
        return lax.rem(z + step, z_count)

    def z_back(step):
        return lax.rem(z + z_count - step, z_count)

    load_keys = pltpu.make_async_copy(key_hbm, keys, local_sem.at[0])
    load_values = pltpu.make_async_copy(value_hbm, values, local_sem.at[1])
    load_weight = pltpu.make_async_copy(weight_hbm, weight, local_sem.at[2])
    load_keys.start()
    load_values.start()
    load_weight.start()

    gq[blk, :, 0:width_q] = q_ref[...]
    gq[blk, :, width_q : width_q + width_kv] = dk_ref[...]
    gq[blk, :, width_q + width_kv :] = dv_ref[...]

    barrier = pltpu.get_barrier_semaphore()
    pl.semaphore_signal(barrier, inc=1, device_id=partner, device_id_type=MESH_ID)
    for step in range(1, z_count):
        pl.semaphore_signal(
            barrier, inc=1, device_id=(kv, z_at(step) * 2 + x), device_id_type=MESH_ID
        )
    for step in range(1, kv_count):
        pl.semaphore_signal(
            barrier, inc=1, device_id=(lax.rem(kv + step, kv_count), blk), device_id_type=MESH_ID
        )
    pl.semaphore_wait(barrier, z_count + kv_count - 1)

    def remote(src, dst, send, recv, device):
        return pltpu.make_async_remote_copy(
            src_ref=src,
            dst_ref=dst,
            send_sem=send,
            recv_sem=recv,
            device_id=device,
            device_id_type=MESH_ID,
        )

    def gather_start(buf, zs, zr, xs, xr):
        here = buf.at[blk]
        remote(here, here, xs.at[0], xr.at[0], partner).start()
        for step in range(1, z_count):
            remote(here, here, zs.at[step], zr.at[step], (kv, z_at(step) * 2 + x)).start()

    def gather_forward(buf, step, zs, zr, xs, xr):
        slot = buf.at[z_back(step) * 2 + x]
        remote(slot, slot, zs.at[step], zr.at[step], partner).wait_recv()
        remote(slot, slot, xs.at[step], xr.at[step], partner).start()

    def gather_wait(buf, step, xs, xr):
        slot = buf.at[z_back(step) * 2 + other]
        remote(slot, slot, xs.at[step], xr.at[step], partner).wait_recv()

    def gather_drain(buf, zs, zr, xs, xr):
        here = buf.at[blk]
        for step in range(z_count):
            remote(here, here, xs.at[step], xr.at[step], partner).wait_send()
            if step:
                remote(here, here, zs.at[step], zr.at[step], partner).wait_send()

    gather_start(gq, gz_send, gz_recv, gx_send, gx_recv)

    node_row = lax.broadcasted_iota(jnp.int32, (TREE_TOKENS, TREE_TOKENS), 0)
    node_col = lax.broadcasted_iota(jnp.int32, (TREE_TOKENS, TREE_TOKENS), 1)
    parent_row = parents_ref[pl.ds(z, 1), :]
    reach = jnp.where(
        (node_row == node_col) | ((parent_row == node_row) & (node_col >= 1)), 1.0, 0.0
    )
    for _ in range((TREE_TOKENS - 1).bit_length()):
        half = reach.astype(jnp.bfloat16)
        reach = jnp.minimum(reach + jnp.dot(half, half, preferred_element_type=jnp.float32), 1.0)
    pick_row = lax.broadcasted_iota(jnp.int32, (TREE_TOKENS, cols), 0)
    pick_col = lax.broadcasted_iota(jnp.int32, (TREE_TOKENS, cols), 1)
    pick = jnp.where(pick_row == x * rows + lax.rem(pick_col, rows), 1.0, 0.0)
    usable = (
        jnp.dot(
            reach.astype(jnp.bfloat16),
            pick.astype(jnp.bfloat16),
            preferred_element_type=jnp.float32,
        )
        > 0.5
    )

    def stacked(slot, group):
        first = group * heads * HEAD_SIZE
        return [
            gq[slot, :, first + h * HEAD_SIZE : first + (h + 1) * HEAD_SIZE] for h in range(heads)
        ]

    def softmax_part(key_rows, value_rows, query_rows, mask):
        scores = (
            lax.dot_general(
                key_rows, query_rows, (((1,), (1,)), ((), ())), preferred_element_type=jnp.float32
            )
            * scale
        )
        scores = jnp.where(mask, scores, -1e30)
        peak = jnp.maximum(jnp.max(scores, axis=0, keepdims=True), ABSENT)
        w = jnp.exp2(scores - peak)
        total = jnp.sum(w, axis=0, keepdims=True)
        out = lax.dot_general(
            value_rows,
            w.astype(jnp.bfloat16),
            (((0,), (0,)), ((), ())),
            preferred_element_type=jnp.float32,
        )
        return out, peak, total

    position = lax.broadcasted_iota(jnp.int32, (block_len, 2 * cols), 0) + blk * block_len

    def cache_step(step):
        request = z_back(step)
        mask = position < len_ref[request]
        for g in range(groups):
            lanes = slice(g * HEAD_SIZE, (g + 1) * HEAD_SIZE)
            query_rows = jnp.concatenate(
                stacked(request * 2 + x, g) + stacked(request * 2 + other, g), axis=0
            )
            out, peak, total = softmax_part(
                keys[request, :, lanes], values[request, :, lanes], query_rows, mask
            )
            own_o[step, g] = out[:, :cols]
            xs_o[step, g] = out[:, cols:].astype(jnp.bfloat16)
            for k, stat in enumerate((peak, total, peak, total)):
                own_st[step, 4 * g + k : 4 * g + k + 1, :] = stat[:, :cols]
                xs_st[step, 4 * g + k : 4 * g + k + 1, :] = stat[:, cols:]
        for copy in x_copies(step):
            copy.start()

    def x_copies(step):
        return (
            remote(xs_o.at[step], xr_o.at[step], x_send.at[step, 0], x_recv.at[step, 0], partner),
            remote(
                xs_st.at[step], xr_st.at[step], x_send.at[step, 1], x_recv.at[step, 1], partner
            ),
        )

    def z_copies(step):
        device = (kv, z_back(step) * 2 + x)
        return (
            remote(zs_o.at[step], zr_o.at[step], z_send.at[step, 0], z_recv.at[step, 0], device),
            remote(zs_st.at[step], zr_st.at[step], z_send.at[step, 1], z_recv.at[step, 1], device),
        )

    def combine(parts):
        peak = parts[0][1]
        for part in parts[1:]:
            peak = jnp.maximum(peak, part[1])
        out = total = None
        for part_out, part_peak, part_total in parts:
            factor = jnp.exp2(part_peak - peak)
            out = part_out * factor if out is None else out + part_out * factor
            total = part_total * factor if total is None else total + part_total * factor
        return out, peak, total

    def merge_step(step):
        for copy in x_copies(step):
            copy.wait_recv()
        for g in range(groups):
            out, peak, total = combine(
                [
                    (own_o[step, g], own_st[step, 4 * g : 4 * g + 1, :], own_st[step, 4 * g + 1 : 4 * g + 2, :]),
                    (
                        xr_o[step, g].astype(jnp.float32),
                        xr_st[step, 4 * g : 4 * g + 1, :],
                        xr_st[step, 4 * g + 1 : 4 * g + 2, :],
                    ),
                ]
            )
            if step == 0:
                own_o[0, g] = out
                own_st[0, 4 * g : 4 * g + 1, :] = peak
                own_st[0, 4 * g + 1 : 4 * g + 2, :] = total
            else:
                zs_o[step, g] = out.astype(jnp.bfloat16)
                for k, stat in enumerate((peak, total, peak, total)):
                    zs_st[step, 4 * g + k : 4 * g + k + 1, :] = stat
        if step:
            for copy in z_copies(step):
                copy.start()

    load_keys.wait()
    load_values.wait()
    gather_forward(gq, 1, gz_send, gz_recv, gx_send, gx_recv)
    gather_wait(gq, 0, gx_send, gx_recv)
    draft_parts = []
    for g in range(groups):
        first = width_q + g * HEAD_SIZE
        tree = gq[pl.ds(z * 2, 2), :, first : first + HEAD_SIZE].reshape(TREE_TOKENS, HEAD_SIZE)
        first += width_kv
        tree_v = gq[pl.ds(z * 2, 2), :, first : first + HEAD_SIZE].reshape(TREE_TOKENS, HEAD_SIZE)
        query_rows = jnp.concatenate(stacked(blk, g), axis=0)
        draft_parts.append(softmax_part(tree, tree_v, query_rows, usable))
    for step in range(2, z_count):
        gather_forward(gq, step, gz_send, gz_recv, gx_send, gx_recv)
    order = list(range(1, z_count)) + [0]
    previous = None
    for step in order:
        if step:
            gather_wait(gq, step, gx_send, gx_recv)
        cache_step(step)
        if previous is not None:
            merge_step(previous)
        previous = step
    merge_step(previous)

    update_row = lax.broadcasted_iota(jnp.int32, (block_len, TREE_TOKENS), 0) + blk * block_len
    update_col = lax.broadcasted_iota(jnp.int32, (block_len, TREE_TOKENS), 1)
    update_wide = lax.broadcasted_iota(jnp.int32, (block_len, width_kv), 0) + blk * block_len
    for r in range(requests):
        length = len_ref[r]
        accepted = count_ref[r]
        offset = update_row - length
        node = jnp.full((block_len, TREE_TOKENS), -1, jnp.int32)
        for k in range(ACC):
            node = jnp.where(offset == k, nodes_ref[r, k], node)
        one_hot = jnp.where((node == update_col) & (offset < accepted), 1.0, 0.0).astype(
            jnp.bfloat16
        )
        wide = update_wide - length
        written = (wide >= 0) & (wide < accepted)
        for cache, first in ((keys, width_q), (values, width_q + width_kv)):
            tree = gq[2 * r : 2 * r + 2, :, first : first + width_kv].reshape(
                TREE_TOKENS, width_kv
            )
            placed = jnp.dot(one_hot, tree, preferred_element_type=jnp.float32)
            cache[r] = jnp.where(written, placed, cache[r].astype(jnp.float32)).astype(
                jnp.bfloat16
            )
    store_keys = pltpu.make_async_copy(keys, new_key_hbm, local_sem.at[3])
    store_values = pltpu.make_async_copy(values, new_value_hbm, local_sem.at[4])
    store_keys.start()
    store_values.start()

    for step in range(1, z_count):
        for copy in z_copies(step):
            copy.wait_recv()
    for g in range(groups):
        low, high = 4 * g, 4 * g + 1
        parts = [draft_parts[g], (own_o[0, g], own_st[0, low : low + 1, :], own_st[0, high : high + 1, :])]
        for step in range(1, z_count):
            parts.append(
                (
                    zr_o[step, g].astype(jnp.float32),
                    zr_st[step, low : low + 1, :],
                    zr_st[step, high : high + 1, :],
                )
            )
        out, _, total = combine(parts)
        turned = (out / total).T.astype(jnp.bfloat16)
        for h in range(heads):
            first = (g * heads + h) * HEAD_SIZE
            ag[blk, :, first : first + HEAD_SIZE] = turned[h * rows : (h + 1) * rows, :]

    gather_start(ag, az_send, az_recv, ax_send, ax_recv)
    load_weight.wait()

    def kv_copy(row_block, source):
        return remote(
            rs_send.at[row_block],
            rs_recv.at[source],
            r_send.at[row_block],
            r_recv.at[source],
            (row_block, blk),
        )

    def project(step):
        row_block = z_back(step)
        lhs = ag[pl.ds(row_block * 2, 2)].reshape(2 * rows, width_q)
        part = jnp.dot(lhs, weight[...], preferred_element_type=jnp.float32)

        @pl.when(row_block == kv)
        def _():
            out_ref[...] = part

        @pl.when(row_block != kv)
        def _():
            rs_send[row_block] = part.astype(jnp.bfloat16)
            kv_copy(row_block, kv).start()

    gather_wait(ag, 0, ax_send, ax_recv)
    gather_forward(ag, 1, az_send, az_recv, ax_send, ax_recv)
    project(0)
    for step in range(2, z_count):
        gather_forward(ag, step, az_send, az_recv, ax_send, ax_recv)
    for step in range(1, z_count):
        gather_wait(ag, step, ax_send, ax_recv)
        project(step)

    gather_drain(gq, gz_send, gz_recv, gx_send, gx_recv)
    gather_drain(ag, az_send, az_recv, ax_send, ax_recv)
    for step in range(z_count):
        for copy in x_copies(step):
            copy.wait_send()
        if step:
            for copy in z_copies(step):
                copy.wait_send()
    store_keys.wait()
    store_values.wait()
    for step in range(1, kv_count):
        peer = lax.rem(kv + step, kv_count)
        copy = kv_copy(peer, peer)
        copy.wait_recv()
        out_ref[...] += rs_recv[peer].astype(jnp.float32)
        copy.wait_send()


def fused(
    queries,
    draft_token_keys,
    draft_token_values,
    cached_key_vectors,
    cached_value_vectors,
    out_weight,
    lengths,
    parents,
    accepted_nodes,
    accepted_count,
):
    blk_count = lax.axis_size("blk")
    kv_count = lax.axis_size("kv")
    z_count = blk_count // 2
    rows, width_q = queries.shape
    width_kv = draft_token_keys.shape[1]
    groups = width_kv // HEAD_SIZE
    cols = rows * (width_q // width_kv)
    out_cols = out_weight.shape[1]
    out_rows = rows * blk_count // kv_count
    bf16, f32 = jnp.bfloat16, jnp.float32
    outs = pltpu.VMEM((z_count, groups, HEAD_SIZE, cols), bf16)
    stats = pltpu.VMEM((z_count, 4 * groups, cols), f32)
    smem = pl.BlockSpec(memory_space=pltpu.SMEM)
    vmem = pl.BlockSpec(memory_space=pltpu.VMEM)
    anywhere = pl.BlockSpec(memory_space=pl.ANY)
    dma = pltpu.SemaphoreType.DMA
    projected, new_keys, new_values = pl.pallas_call(
        functools.partial(fused_kernel, z_count, kv_count),
        out_shape=(
            jax.ShapeDtypeStruct((out_rows, out_cols), f32),
            jax.ShapeDtypeStruct(cached_key_vectors.shape, bf16),
            jax.ShapeDtypeStruct(cached_value_vectors.shape, bf16),
        ),
        in_specs=[smem] * 3 + [vmem] * 4 + [anywhere] * 3,
        out_specs=(vmem, anywhere, anywhere),
        scratch_shapes=[
            pltpu.VMEM((blk_count, rows, width_q + 2 * width_kv), bf16),
            pltpu.VMEM(cached_key_vectors.shape, bf16),
            pltpu.VMEM(cached_value_vectors.shape, bf16),
            pltpu.VMEM(out_weight.shape, bf16),
            pltpu.VMEM((z_count, groups, HEAD_SIZE, cols), f32),
            stats,
            outs,
            stats,
            outs,
            stats,
            outs,
            stats,
            outs,
            stats,
            pltpu.VMEM((blk_count, rows, width_q), bf16),
            pltpu.VMEM((kv_count, out_rows, out_cols), bf16),
            pltpu.VMEM((kv_count, out_rows, out_cols), bf16),
            dma((5,)),
        ]
        + [dma((z_count,))] * 4
        + [dma((z_count, 2))] * 4
        + [dma((z_count,))] * 4
        + [dma((kv_count,))] * 2,
        compiler_params=pltpu.CompilerParams(
            collective_id=0, has_side_effects=True, vmem_limit_bytes=48 * 1024 * 1024
        ),
        cost_estimate=pl.CostEstimate(
            flops=4 * 10**9, bytes_accessed=9 * 10**6, transcendentals=2 * 10**6
        ),
    )(
        lengths,
        accepted_count,
        accepted_nodes,
        parents,
        queries,
        draft_token_keys,
        draft_token_values,
        cached_key_vectors,
        cached_value_vectors,
        out_weight,
    )
    return (projected.astype(bf16), new_keys, new_values)


def solution(mesh):
    kv_count, blk_count = mesh.shape["kv"], mesh.shape["blk"]
    paired = kv_count * 2 == blk_count and kv_count <= 4
    return jax.shard_map(
        fused if paired else on_device,
        mesh=mesh,
        in_specs=(
            P("blk", "kv"),
            P("blk", "kv"),
            P("blk", "kv"),
            P(None, "blk", "kv"),
            P(None, "blk", "kv"),
            P("kv", "blk"),
            P(),
            P(),
            P(),
            P(),
        ),
        out_specs=(P("kv", "blk"), P(None, "blk", "kv"), P(None, "blk", "kv")),
        check_vma=False,
    )
```

```python
import functools
import math

import jax
import jax.numpy as jnp
from jax import lax
from jax.experimental import pallas as pl
from jax.experimental.pallas import tpu as pltpu
from jax.sharding import PartitionSpec as P

HEAD_SIZE = 128
TREE_TOKENS = 64
ACC = 8


NEG_FLOOR = -1e30


def ancestors(parent_rows):
    node_ids = jnp.arange(TREE_TOKENS, dtype=jnp.int32)
    parent_link = (
        (parent_rows[:, :, None] == node_ids[None, None, :]) & (node_ids[None, :, None] >= 1)
    ).astype(jnp.float32)
    reachable = jnp.eye(TREE_TOKENS, dtype=jnp.float32)[None] + parent_link
    for doubling in range((TREE_TOKENS - 1).bit_length()):
        reachable = jnp.minimum(
            reachable
            + jnp.einsum("rij,rjk->rik", reachable, reachable, precision=lax.Precision.HIGHEST),
            1.0,
        )
    return reachable


def partial_softmax(query_vectors, key_rows, value_rows, usable, score_scale):
    scores = (
        jnp.einsum(
            "rtkgh,rbpkh->brkgtp", query_vectors, key_rows, preferred_element_type=jnp.float32
        )
        * score_scale
    )
    scores = jnp.where(usable, scores, NEG_FLOOR)
    peak_score = jnp.max(scores, axis=-1)
    weights = jnp.where(usable, jnp.exp(scores - peak_score[..., None]), 0.0)
    weight_sum = jnp.sum(weights, axis=-1)
    weighted = jnp.einsum(
        "brkgtp,rbpkh->brtkgh",
        weights.astype(jnp.bfloat16),
        value_rows,
        preferred_element_type=jnp.float32,
    )
    block_count, req_count, kv_count, query_group_width, row_count = peak_score.shape
    weighted = weighted.reshape(
        block_count, req_count * row_count, kv_count * query_group_width * value_rows.shape[-1]
    )
    peak_score = peak_score.transpose(0, 1, 4, 2, 3).reshape(
        block_count, req_count * row_count, kv_count * query_group_width
    )
    weight_sum = weight_sum.transpose(0, 1, 4, 2, 3).reshape(
        block_count, req_count * row_count, kv_count * query_group_width
    )
    return (weighted, peak_score, weight_sum)


def merge_parts(cache_part, draft_part, head_dim):
    cache_out, cache_peak, cache_sum = cache_part
    draft_out, draft_peak, draft_sum = draft_part
    cache_out = cache_out.astype(jnp.float32)
    overall = jnp.maximum(jnp.max(cache_peak, axis=0), draft_peak[0])
    cache_factor = jnp.exp(cache_peak - overall[None])
    draft_factor = jnp.exp(draft_peak[0] - overall)
    denominator = jnp.sum(cache_factor * cache_sum, axis=0) + draft_factor * draft_sum[0]
    block_count, row_count, head_count = cache_peak.shape
    numerator = jnp.sum(
        cache_factor[..., None] * cache_out.reshape(block_count, row_count, head_count, head_dim),
        axis=0,
    )
    numerator = numerator + draft_factor[..., None] * draft_out[0].reshape(
        row_count, head_count, head_dim
    )
    return (
        (numerator / denominator[..., None])
        .reshape(row_count, head_count * head_dim)
        .astype(jnp.bfloat16)
    )


def place_rows(sources, slot_index, written, cache_rows):
    slot_ids = jnp.arange(sources.shape[1], dtype=jnp.int32)
    selector = ((slot_index[:, :, None] == slot_ids[None, None, :]) & written[:, :, None]).astype(
        jnp.bfloat16
    )
    placed = jnp.einsum(
        "rps,rsc->rpc", selector, sources, preferred_element_type=jnp.float32
    ).astype(jnp.bfloat16)
    return jnp.where(written[:, :, None], placed, cache_rows)


def on_device(
    queries,
    draft_token_keys,
    draft_token_values,
    cached_key_vectors,
    cached_value_vectors,
    out_weight,
    lengths,
    parents,
    accepted_nodes,
    accepted_count,
):
    block_count = lax.axis_size("blk")
    my_block = lax.axis_index("blk")
    rows_dev, width_q = queries.shape
    requests = lengths.shape[0]
    cache_width = cached_key_vectors.shape[2]
    kv_local = cache_width // HEAD_SIZE
    query_group_width = width_q // (kv_local * HEAD_SIZE)
    block_len = cached_key_vectors.shape[1]
    score_scale = 1.0 / math.sqrt(HEAD_SIZE)
    leading_row = my_block * rows_dev
    my_request = leading_row // TREE_TOKENS
    node_start = leading_row - my_request * TREE_TOKENS
    local_queries = queries.reshape(1, rows_dev, kv_local, query_group_width, HEAD_SIZE)
    gathered_keys, gathered_values = (
        lax.all_gather(draft_token_keys, "blk", axis=0, tiled=True),
        lax.all_gather(draft_token_values, "blk", axis=0, tiled=True),
    )
    tree_keys = lax.dynamic_slice_in_dim(
        gathered_keys, my_request * TREE_TOKENS, TREE_TOKENS, 0
    ).reshape(1, 1, TREE_TOKENS, kv_local, HEAD_SIZE)
    tree_values = lax.dynamic_slice_in_dim(
        gathered_values, my_request * TREE_TOKENS, TREE_TOKENS, 0
    ).reshape(1, 1, TREE_TOKENS, kv_local, HEAD_SIZE)
    reachable = ancestors(lax.dynamic_slice_in_dim(parents, my_request, 1, 0))
    own_reach = lax.dynamic_slice_in_dim(reachable, node_start, rows_dev, 1)
    draft_usable = (own_reach > 0.5)[None, :, None, None, :, :]
    draft_part = partial_softmax(local_queries, tree_keys, tree_values, draft_usable, score_scale)
    every_query = lax.all_gather(queries, "blk", axis=0, tiled=True)
    all_queries = every_query.reshape(requests, TREE_TOKENS, kv_local, query_group_width, HEAD_SIZE)
    positions = my_block * block_len + jnp.arange(block_len, dtype=jnp.int32)
    usable = (positions[None, :] < lengths[:, None])[None, :, None, None, None, :]
    local_out, local_peak, local_sum = partial_softmax(
        all_queries,
        cached_key_vectors.reshape(requests, 1, block_len, kv_local, HEAD_SIZE),
        cached_value_vectors.reshape(requests, 1, block_len, kv_local, HEAD_SIZE),
        usable,
        score_scale,
    )
    moved_out = lax.all_to_all(
        local_out[0].astype(jnp.bfloat16), "blk", split_axis=0, concat_axis=0, tiled=True
    )
    moved_peak, moved_sum = (
        lax.all_to_all(local_peak[0], "blk", split_axis=0, concat_axis=0, tiled=True),
        lax.all_to_all(local_sum[0], "blk", split_axis=0, concat_axis=0, tiled=True),
    )
    cache_part = (
        moved_out.reshape(block_count, rows_dev, -1),
        moved_peak.reshape(block_count, rows_dev, -1),
        moved_sum.reshape(block_count, rows_dev, -1),
    )
    attention = merge_parts(cache_part, draft_part, HEAD_SIZE)
    every_row = lax.all_gather(attention, "blk", axis=0, tiled=True)
    projected = lax.psum_scatter(
        jnp.dot(every_row, out_weight, preferred_element_type=jnp.float32),
        "kv",
        scatter_dimension=0,
        tiled=True,
    ).astype(jnp.bfloat16)
    positions_here = my_block * block_len + jnp.arange(block_len, dtype=jnp.int32)
    offset = positions_here[None, :] - lengths[:, None]
    written = (offset >= 0) & (offset < accepted_count[:, None])
    slot_match = offset[:, :, None] == jnp.arange(ACC, dtype=jnp.int32)[None, None, :]
    node_ids = jnp.sum(jnp.where(slot_match, accepted_nodes[:, None, :], 0), axis=-1)
    new_cache_keys = place_rows(
        gathered_keys.reshape(requests, TREE_TOKENS, cache_width),
        node_ids,
        written,
        cached_key_vectors,
    )
    new_cache_values = place_rows(
        gathered_values.reshape(requests, TREE_TOKENS, cache_width),
        node_ids,
        written,
        cached_value_vectors,
    )
    return (projected, new_cache_keys, new_cache_values)


LOG2E = 1.4426950408889634
MESH_ID = pl.DeviceIdType.MESH
ABSENT = -1e20


def fused_kernel(
    z_count,
    kv_count,
    len_hbm,
    count_hbm,
    nodes_hbm,
    parents_hbm,
    q_hbm,
    dk_hbm,
    dv_hbm,
    key_hbm,
    value_hbm,
    weight_hbm,
    out_ref,
    new_key_hbm,
    new_value_hbm,
    len_ref,
    count_ref,
    nodes_ref,
    parents_ref,
    gq,
    tree,
    picked,
    keys,
    values,
    weight,
    own_o,
    own_st,
    xs_o,
    xs_st,
    xr_o,
    xr_st,
    zs_o,
    zs_st,
    zr_o,
    zr_st,
    ag,
    rs_send,
    rs_recv,
    local_sem,
    gz_send,
    gz_recv,
    gx_send,
    gx_recv,
    t_send,
    t_recv,
    p_send,
    p_recv,
    x_send,
    x_recv,
    z_send,
    z_recv,
    az_send,
    az_recv,
    ax_send,
    ax_recv,
    r_send,
    r_recv,
):
    kv = lax.axis_index("kv")
    blk = lax.axis_index("blk")
    z = blk // 2
    x = blk % 2
    other = 1 - x
    partner = (kv, z * 2 + other)
    rows, width_q = q_hbm.shape
    width_kv = dk_hbm.shape[1]
    groups = width_kv // HEAD_SIZE
    heads = width_q // width_kv
    cols = rows * heads
    requests, block_len, _ = keys.shape
    scale = LOG2E / math.sqrt(HEAD_SIZE)

    def z_at(step):
        return lax.rem(z + step, z_count)

    def z_back(step):
        return lax.rem(z + z_count - step, z_count)

    load_keys = pltpu.make_async_copy(key_hbm, keys, local_sem.at[0])
    load_values = pltpu.make_async_copy(value_hbm, values, local_sem.at[1])
    load_weight = pltpu.make_async_copy(weight_hbm, weight, local_sem.at[2])
    first_loads = [
        pltpu.make_async_copy(src, dst, local_sem.at[5 + i])
        for i, (src, dst) in enumerate(
            (
                (q_hbm, gq.at[blk]),
                (dk_hbm, tree.at[0, x]),
                (dv_hbm, tree.at[1, x]),
                (parents_hbm, parents_ref),
                (nodes_hbm, nodes_ref),
                (len_hbm, len_ref),
                (count_hbm, count_ref),
            )
        )
    ]
    for load in first_loads:
        load.start()
    load_keys.start()
    load_values.start()
    load_weight.start()

    barrier = pltpu.get_barrier_semaphore()
    pl.semaphore_signal(barrier, inc=1, device_id=partner, device_id_type=MESH_ID)
    for step in range(1, z_count):
        pl.semaphore_signal(
            barrier, inc=1, device_id=(kv, z_at(step) * 2 + x), device_id_type=MESH_ID
        )
    for step in range(1, kv_count):
        pl.semaphore_signal(
            barrier, inc=1, device_id=(lax.rem(kv + step, kv_count), blk), device_id_type=MESH_ID
        )
    pl.semaphore_wait(barrier, z_count + kv_count - 1)

    def remote(src, dst, send, recv, device):
        return pltpu.make_async_remote_copy(
            src_ref=src,
            dst_ref=dst,
            send_sem=send,
            recv_sem=recv,
            device_id=device,
            device_id_type=MESH_ID,
        )

    def gather_start(buf, zs, zr, xs, xr):
        here = buf.at[blk]
        remote(here, here, xs.at[0], xr.at[0], partner).start()
        for step in range(1, z_count):
            remote(here, here, zs.at[step], zr.at[step], (kv, z_at(step) * 2 + x)).start()

    def gather_forward(buf, step, zs, zr, xs, xr):
        slot = buf.at[z_back(step) * 2 + x]
        remote(slot, slot, zs.at[step], zr.at[step], partner).wait_recv()
        remote(slot, slot, xs.at[step], xr.at[step], partner).start()

    def gather_wait(buf, step, xs, xr):
        slot = buf.at[z_back(step) * 2 + other]
        remote(slot, slot, xs.at[step], xr.at[step], partner).wait_recv()

    def gather_drain(buf, zs, zr, xs, xr):
        here = buf.at[blk]
        for step in range(z_count):
            remote(here, here, xs.at[step], xr.at[step], partner).wait_send()
            if step:
                remote(here, here, zs.at[step], zr.at[step], partner).wait_send()

    def tree_copy(which):
        own = tree.at[which, x]
        return remote(own, own, t_send.at[which], t_recv.at[which], partner)

    def picked_copy(step):
        own = picked.at[z]
        return remote(own, own, p_send.at[step], p_recv.at[step], (kv, z_at(step) * 2 + x))

    for load in first_loads[:3]:
        load.wait()
    gather_start(gq, gz_send, gz_recv, gx_send, gx_recv)
    for which in range(2):
        tree_copy(which).start()
    for load in first_loads[3:]:
        load.wait()

    node_row = lax.broadcasted_iota(jnp.int32, (TREE_TOKENS, TREE_TOKENS), 0)
    node_col = lax.broadcasted_iota(jnp.int32, (TREE_TOKENS, TREE_TOKENS), 1)
    parent_row = parents_ref[pl.ds(z, 1), :]
    reach = jnp.where(
        (node_row == node_col) | ((parent_row == node_row) & (node_col >= 1)), 1.0, 0.0
    )
    for _ in range((TREE_TOKENS - 1).bit_length()):
        half = reach.astype(jnp.bfloat16)
        reach = jnp.minimum(reach + jnp.dot(half, half, preferred_element_type=jnp.float32), 1.0)
    pick_row = lax.broadcasted_iota(jnp.int32, (TREE_TOKENS, cols), 0)
    pick_col = lax.broadcasted_iota(jnp.int32, (TREE_TOKENS, cols), 1)
    pick = jnp.where(pick_row == x * rows + lax.rem(pick_col, rows), 1.0, 0.0)
    usable = (
        jnp.dot(
            reach.astype(jnp.bfloat16),
            pick.astype(jnp.bfloat16),
            preferred_element_type=jnp.float32,
        )
        > 0.5
    )

    def stacked(slot, group):
        first = group * heads * HEAD_SIZE
        return [
            gq[slot, :, first + h * HEAD_SIZE : first + (h + 1) * HEAD_SIZE] for h in range(heads)
        ]

    def softmax_part(key_rows, value_rows, query_rows, mask):
        scores = (
            lax.dot_general(
                key_rows, query_rows, (((1,), (1,)), ((), ())), preferred_element_type=jnp.float32
            )
            * scale
        )
        scores = jnp.where(mask, scores, -1e30)
        peak = jnp.maximum(jnp.max(scores, axis=0, keepdims=True), ABSENT)
        w = jnp.exp2(scores - peak)
        total = jnp.sum(w, axis=0, keepdims=True)
        out = lax.dot_general(
            value_rows,
            w.astype(jnp.bfloat16),
            (((0,), (0,)), ((), ())),
            preferred_element_type=jnp.float32,
        )
        return out, peak, total

    position = lax.broadcasted_iota(jnp.int32, (block_len, 2 * cols), 0) + blk * block_len

    def cache_step(step):
        request = z_back(step)
        mask = position < len_ref[request]
        for g in range(groups):
            lanes = slice(g * HEAD_SIZE, (g + 1) * HEAD_SIZE)
            query_rows = jnp.concatenate(
                stacked(request * 2 + x, g) + stacked(request * 2 + other, g), axis=0
            )
            out, peak, total = softmax_part(
                keys[request, :, lanes], values[request, :, lanes], query_rows, mask
            )
            own_o[step, g] = out[:, :cols]
            xs_o[step, g] = out[:, cols:].astype(jnp.bfloat16)
            for k, stat in enumerate((peak, total, peak, total)):
                own_st[step, 4 * g + k : 4 * g + k + 1, :] = stat[:, :cols]
                xs_st[step, 4 * g + k : 4 * g + k + 1, :] = stat[:, cols:]
        for copy in x_copies(step):
            copy.start()

    def x_copies(step):
        return (
            remote(xs_o.at[step], xr_o.at[step], x_send.at[step, 0], x_recv.at[step, 0], partner),
            remote(
                xs_st.at[step], xr_st.at[step], x_send.at[step, 1], x_recv.at[step, 1], partner
            ),
        )

    def z_copies(step):
        device = (kv, z_back(step) * 2 + x)
        return (
            remote(zs_o.at[step], zr_o.at[step], z_send.at[step, 0], z_recv.at[step, 0], device),
            remote(zs_st.at[step], zr_st.at[step], z_send.at[step, 1], z_recv.at[step, 1], device),
        )

    def combine(parts):
        peak = parts[0][1]
        for part in parts[1:]:
            peak = jnp.maximum(peak, part[1])
        out = total = None
        for part_out, part_peak, part_total in parts:
            factor = jnp.exp2(part_peak - peak)
            out = part_out * factor if out is None else out + part_out * factor
            total = part_total * factor if total is None else total + part_total * factor
        return out, peak, total

    def merge_step(step):
        for copy in x_copies(step):
            copy.wait_recv()
        for g in range(groups):
            out, peak, total = combine(
                [
                    (own_o[step, g], own_st[step, 4 * g : 4 * g + 1, :], own_st[step, 4 * g + 1 : 4 * g + 2, :]),
                    (
                        xr_o[step, g].astype(jnp.float32),
                        xr_st[step, 4 * g : 4 * g + 1, :],
                        xr_st[step, 4 * g + 1 : 4 * g + 2, :],
                    ),
                ]
            )
            if step == 0:
                own_o[0, g] = out
                own_st[0, 4 * g : 4 * g + 1, :] = peak
                own_st[0, 4 * g + 1 : 4 * g + 2, :] = total
            else:
                zs_o[step, g] = out.astype(jnp.bfloat16)
                for k, stat in enumerate((peak, total, peak, total)):
                    zs_st[step, 4 * g + k : 4 * g + k + 1, :] = stat
        if step:
            for copy in z_copies(step):
                copy.start()

    load_keys.wait()
    load_values.wait()
    gather_forward(gq, 1, gz_send, gz_recv, gx_send, gx_recv)
    gather_wait(gq, 0, gx_send, gx_recv)
    for which in range(2):
        tree_copy(which).wait_recv()
    slot_row = lax.broadcasted_iota(jnp.int32, (ACC, TREE_TOKENS), 0)
    slot_col = lax.broadcasted_iota(jnp.int32, (ACC, TREE_TOKENS), 1)
    node = jnp.zeros((ACC, TREE_TOKENS), jnp.int32)
    for k in range(ACC):
        node = jnp.where(slot_row == k, nodes_ref[z, k], node)
    one_hot = jnp.where(node == slot_col, 1.0, 0.0).astype(jnp.bfloat16)
    picked[z] = jnp.concatenate(
        [
            jnp.dot(
                one_hot,
                tree[which].reshape(TREE_TOKENS, width_kv),
                preferred_element_type=jnp.float32,
            )
            for which in range(2)
        ],
        axis=0,
    ).astype(jnp.bfloat16)
    for step in range(1, z_count):
        picked_copy(step).start()
    draft_parts = []
    for g in range(groups):
        lanes = slice(g * HEAD_SIZE, (g + 1) * HEAD_SIZE)
        tree_k = tree[0, :, :, lanes].reshape(TREE_TOKENS, HEAD_SIZE)
        tree_v = tree[1, :, :, lanes].reshape(TREE_TOKENS, HEAD_SIZE)
        query_rows = jnp.concatenate(stacked(blk, g), axis=0)
        draft_parts.append(softmax_part(tree_k, tree_v, query_rows, usable))
    for step in range(2, z_count):
        gather_forward(gq, step, gz_send, gz_recv, gx_send, gx_recv)
    order = list(range(1, z_count)) + [0]
    previous = None
    for step in order:
        if step:
            gather_wait(gq, step, gx_send, gx_recv)
        cache_step(step)
        if previous is not None:
            merge_step(previous)
        previous = step
    merge_step(previous)

    for step in range(1, z_count):
        picked_copy(step).wait_recv()
    update_row = lax.broadcasted_iota(jnp.int32, (block_len, 2 * ACC), 0) + blk * block_len
    update_col = lax.broadcasted_iota(jnp.int32, (block_len, 2 * ACC), 1)
    update_wide = lax.broadcasted_iota(jnp.int32, (block_len, width_kv), 0) + blk * block_len
    for r in range(requests):
        wide = update_wide - len_ref[r]
        written = (wide >= 0) & (wide < count_ref[r])
        for which, cache in enumerate((keys, values)):
            offset = update_row - len_ref[r]
            one_hot = jnp.where(
                (offset + which * ACC == update_col) & (offset >= 0) & (offset < ACC), 1.0, 0.0
            )
            placed = jnp.dot(
                one_hot.astype(jnp.bfloat16), picked[r], preferred_element_type=jnp.float32
            )
            cache[r] = jnp.where(written, placed, cache[r].astype(jnp.float32)).astype(
                jnp.bfloat16
            )
    store_keys = pltpu.make_async_copy(keys, new_key_hbm, local_sem.at[3])
    store_values = pltpu.make_async_copy(values, new_value_hbm, local_sem.at[4])
    store_keys.start()
    store_values.start()

    for step in range(1, z_count):
        for copy in z_copies(step):
            copy.wait_recv()
    for g in range(groups):
        low, high = 4 * g, 4 * g + 1
        parts = [draft_parts[g], (own_o[0, g], own_st[0, low : low + 1, :], own_st[0, high : high + 1, :])]
        for step in range(1, z_count):
            parts.append(
                (
                    zr_o[step, g].astype(jnp.float32),
                    zr_st[step, low : low + 1, :],
                    zr_st[step, high : high + 1, :],
                )
            )
        out, _, total = combine(parts)
        turned = (out / total).T.astype(jnp.bfloat16)
        for h in range(heads):
            first = (g * heads + h) * HEAD_SIZE
            ag[blk, :, first : first + HEAD_SIZE] = turned[h * rows : (h + 1) * rows, :]

    gather_start(ag, az_send, az_recv, ax_send, ax_recv)
    load_weight.wait()

    def kv_copy(row_block, source):
        return remote(
            rs_send.at[row_block],
            rs_recv.at[source],
            r_send.at[row_block],
            r_recv.at[source],
            (row_block, blk),
        )

    def project(step):
        row_block = z_back(step)
        lhs = ag[pl.ds(row_block * 2, 2)].reshape(2 * rows, width_q)
        part = jnp.dot(lhs, weight[...], preferred_element_type=jnp.float32)

        @pl.when(row_block == kv)
        def _():
            out_ref[...] = part

        @pl.when(row_block != kv)
        def _():
            rs_send[row_block] = part.astype(jnp.bfloat16)
            kv_copy(row_block, kv).start()

    gather_wait(ag, 0, ax_send, ax_recv)
    gather_forward(ag, 1, az_send, az_recv, ax_send, ax_recv)
    project(0)
    for step in range(2, z_count):
        gather_forward(ag, step, az_send, az_recv, ax_send, ax_recv)
    for step in range(1, z_count):
        gather_wait(ag, step, ax_send, ax_recv)
        project(step)

    gather_drain(gq, gz_send, gz_recv, gx_send, gx_recv)
    gather_drain(ag, az_send, az_recv, ax_send, ax_recv)
    for step in range(z_count):
        for copy in x_copies(step):
            copy.wait_send()
        if step:
            for copy in z_copies(step):
                copy.wait_send()
    for which in range(2):
        tree_copy(which).wait_send()
    for step in range(1, z_count):
        picked_copy(step).wait_send()
    store_keys.wait()
    store_values.wait()
    for step in range(1, kv_count):
        peer = lax.rem(kv + step, kv_count)
        copy = kv_copy(peer, peer)
        copy.wait_recv()
        out_ref[...] += rs_recv[peer].astype(jnp.float32)
        copy.wait_send()


def fused(
    queries,
    draft_token_keys,
    draft_token_values,
    cached_key_vectors,
    cached_value_vectors,
    out_weight,
    lengths,
    parents,
    accepted_nodes,
    accepted_count,
):
    blk_count = lax.axis_size("blk")
    kv_count = lax.axis_size("kv")
    z_count = blk_count // 2
    rows, width_q = queries.shape
    width_kv = draft_token_keys.shape[1]
    groups = width_kv // HEAD_SIZE
    cols = rows * (width_q // width_kv)
    out_cols = out_weight.shape[1]
    out_rows = rows * blk_count // kv_count
    bf16, f32 = jnp.bfloat16, jnp.float32
    outs = pltpu.VMEM((z_count, groups, HEAD_SIZE, cols), bf16)
    stats = pltpu.VMEM((z_count, 4 * groups, cols), f32)
    vmem = pl.BlockSpec(memory_space=pltpu.VMEM)
    hbm = pl.BlockSpec(memory_space=pltpu.HBM)
    dma = pltpu.SemaphoreType.DMA
    projected, new_keys, new_values = pl.pallas_call(
        functools.partial(fused_kernel, z_count, kv_count),
        out_shape=(
            jax.ShapeDtypeStruct((out_rows, out_cols), f32),
            jax.ShapeDtypeStruct(cached_key_vectors.shape, bf16),
            jax.ShapeDtypeStruct(cached_value_vectors.shape, bf16),
        ),
        in_specs=[hbm] * 10,
        out_specs=(vmem, hbm, hbm),
        scratch_shapes=[
            pltpu.SMEM(lengths.shape, jnp.int32),
            pltpu.SMEM(accepted_count.shape, jnp.int32),
            pltpu.SMEM(accepted_nodes.shape, jnp.int32),
            pltpu.VMEM(parents.shape, jnp.int32),
            pltpu.VMEM((blk_count, rows, width_q), bf16),
            pltpu.VMEM((2, 2, rows, width_kv), bf16),
            pltpu.VMEM((z_count, 2 * ACC, width_kv), bf16),
            pltpu.VMEM(cached_key_vectors.shape, bf16),
            pltpu.VMEM(cached_value_vectors.shape, bf16),
            pltpu.VMEM(out_weight.shape, bf16),
            pltpu.VMEM((z_count, groups, HEAD_SIZE, cols), f32),
            stats,
            outs,
            stats,
            outs,
            stats,
            outs,
            stats,
            outs,
            stats,
            pltpu.VMEM((blk_count, rows, width_q), bf16),
            pltpu.VMEM((kv_count, out_rows, out_cols), bf16),
            pltpu.VMEM((kv_count, out_rows, out_cols), bf16),
            dma((12,)),
        ]
        + [dma((z_count,))] * 4
        + [dma((2,))] * 2
        + [dma((z_count,))] * 2
        + [dma((z_count, 2))] * 4
        + [dma((z_count,))] * 4
        + [dma((kv_count,))] * 2,
        compiler_params=pltpu.CompilerParams(
            collective_id=0, has_side_effects=True, vmem_limit_bytes=63 * 1024 * 1024
        ),
        cost_estimate=pl.CostEstimate(
            flops=4 * 10**9, bytes_accessed=9 * 10**6, transcendentals=2 * 10**6
        ),
    )(
        lengths,
        accepted_count,
        accepted_nodes,
        parents,
        queries,
        draft_token_keys,
        draft_token_values,
        cached_key_vectors,
        cached_value_vectors,
        out_weight,
    )
    return (projected.astype(bf16), new_keys, new_values)


def solution(mesh):
    kv_count, blk_count = mesh.shape["kv"], mesh.shape["blk"]
    paired = kv_count * 2 == blk_count and kv_count <= 4
    return jax.shard_map(
        fused if paired else on_device,
        mesh=mesh,
        in_specs=(
            P("blk", "kv"),
            P("blk", "kv"),
            P("blk", "kv"),
            P(None, "blk", "kv"),
            P(None, "blk", "kv"),
            P("kv", "blk"),
            P(),
            P(),
            P(),
            P(),
        ),
        out_specs=(P("kv", "blk"), P(None, "blk", "kv"), P(None, "blk", "kv")),
        check_vma=False,
    )
```

```python
import functools
import math

import jax
import jax.numpy as jnp
from jax import lax
from jax.experimental import pallas as pl
from jax.experimental.pallas import tpu as pltpu
from jax.sharding import PartitionSpec as P

HEAD_SIZE = 128
TREE_TOKENS = 64
ACC = 8


NEG_FLOOR = -1e30


def ancestors(parent_rows):
    node_ids = jnp.arange(TREE_TOKENS, dtype=jnp.int32)
    parent_link = (
        (parent_rows[:, :, None] == node_ids[None, None, :]) & (node_ids[None, :, None] >= 1)
    ).astype(jnp.float32)
    reachable = jnp.eye(TREE_TOKENS, dtype=jnp.float32)[None] + parent_link
    for doubling in range((TREE_TOKENS - 1).bit_length()):
        reachable = jnp.minimum(
            reachable
            + jnp.einsum("rij,rjk->rik", reachable, reachable, precision=lax.Precision.HIGHEST),
            1.0,
        )
    return reachable


def partial_softmax(query_vectors, key_rows, value_rows, usable, score_scale):
    scores = (
        jnp.einsum(
            "rtkgh,rbpkh->brkgtp", query_vectors, key_rows, preferred_element_type=jnp.float32
        )
        * score_scale
    )
    scores = jnp.where(usable, scores, NEG_FLOOR)
    peak_score = jnp.max(scores, axis=-1)
    weights = jnp.where(usable, jnp.exp(scores - peak_score[..., None]), 0.0)
    weight_sum = jnp.sum(weights, axis=-1)
    weighted = jnp.einsum(
        "brkgtp,rbpkh->brtkgh",
        weights.astype(jnp.bfloat16),
        value_rows,
        preferred_element_type=jnp.float32,
    )
    block_count, req_count, kv_count, query_group_width, row_count = peak_score.shape
    weighted = weighted.reshape(
        block_count, req_count * row_count, kv_count * query_group_width * value_rows.shape[-1]
    )
    peak_score = peak_score.transpose(0, 1, 4, 2, 3).reshape(
        block_count, req_count * row_count, kv_count * query_group_width
    )
    weight_sum = weight_sum.transpose(0, 1, 4, 2, 3).reshape(
        block_count, req_count * row_count, kv_count * query_group_width
    )
    return (weighted, peak_score, weight_sum)


def merge_parts(cache_part, draft_part, head_dim):
    cache_out, cache_peak, cache_sum = cache_part
    draft_out, draft_peak, draft_sum = draft_part
    cache_out = cache_out.astype(jnp.float32)
    overall = jnp.maximum(jnp.max(cache_peak, axis=0), draft_peak[0])
    cache_factor = jnp.exp(cache_peak - overall[None])
    draft_factor = jnp.exp(draft_peak[0] - overall)
    denominator = jnp.sum(cache_factor * cache_sum, axis=0) + draft_factor * draft_sum[0]
    block_count, row_count, head_count = cache_peak.shape
    numerator = jnp.sum(
        cache_factor[..., None] * cache_out.reshape(block_count, row_count, head_count, head_dim),
        axis=0,
    )
    numerator = numerator + draft_factor[..., None] * draft_out[0].reshape(
        row_count, head_count, head_dim
    )
    return (
        (numerator / denominator[..., None])
        .reshape(row_count, head_count * head_dim)
        .astype(jnp.bfloat16)
    )


def place_rows(sources, slot_index, written, cache_rows):
    slot_ids = jnp.arange(sources.shape[1], dtype=jnp.int32)
    selector = ((slot_index[:, :, None] == slot_ids[None, None, :]) & written[:, :, None]).astype(
        jnp.bfloat16
    )
    placed = jnp.einsum(
        "rps,rsc->rpc", selector, sources, preferred_element_type=jnp.float32
    ).astype(jnp.bfloat16)
    return jnp.where(written[:, :, None], placed, cache_rows)


def on_device(
    queries,
    draft_token_keys,
    draft_token_values,
    cached_key_vectors,
    cached_value_vectors,
    out_weight,
    lengths,
    parents,
    accepted_nodes,
    accepted_count,
):
    block_count = lax.axis_size("blk")
    my_block = lax.axis_index("blk")
    rows_dev, width_q = queries.shape
    requests = lengths.shape[0]
    cache_width = cached_key_vectors.shape[2]
    kv_local = cache_width // HEAD_SIZE
    query_group_width = width_q // (kv_local * HEAD_SIZE)
    block_len = cached_key_vectors.shape[1]
    score_scale = 1.0 / math.sqrt(HEAD_SIZE)
    leading_row = my_block * rows_dev
    my_request = leading_row // TREE_TOKENS
    node_start = leading_row - my_request * TREE_TOKENS
    local_queries = queries.reshape(1, rows_dev, kv_local, query_group_width, HEAD_SIZE)
    gathered_keys, gathered_values = (
        lax.all_gather(draft_token_keys, "blk", axis=0, tiled=True),
        lax.all_gather(draft_token_values, "blk", axis=0, tiled=True),
    )
    tree_keys = lax.dynamic_slice_in_dim(
        gathered_keys, my_request * TREE_TOKENS, TREE_TOKENS, 0
    ).reshape(1, 1, TREE_TOKENS, kv_local, HEAD_SIZE)
    tree_values = lax.dynamic_slice_in_dim(
        gathered_values, my_request * TREE_TOKENS, TREE_TOKENS, 0
    ).reshape(1, 1, TREE_TOKENS, kv_local, HEAD_SIZE)
    reachable = ancestors(lax.dynamic_slice_in_dim(parents, my_request, 1, 0))
    own_reach = lax.dynamic_slice_in_dim(reachable, node_start, rows_dev, 1)
    draft_usable = (own_reach > 0.5)[None, :, None, None, :, :]
    draft_part = partial_softmax(local_queries, tree_keys, tree_values, draft_usable, score_scale)
    every_query = lax.all_gather(queries, "blk", axis=0, tiled=True)
    all_queries = every_query.reshape(requests, TREE_TOKENS, kv_local, query_group_width, HEAD_SIZE)
    positions = my_block * block_len + jnp.arange(block_len, dtype=jnp.int32)
    usable = (positions[None, :] < lengths[:, None])[None, :, None, None, None, :]
    local_out, local_peak, local_sum = partial_softmax(
        all_queries,
        cached_key_vectors.reshape(requests, 1, block_len, kv_local, HEAD_SIZE),
        cached_value_vectors.reshape(requests, 1, block_len, kv_local, HEAD_SIZE),
        usable,
        score_scale,
    )
    moved_out = lax.all_to_all(
        local_out[0].astype(jnp.bfloat16), "blk", split_axis=0, concat_axis=0, tiled=True
    )
    moved_peak, moved_sum = (
        lax.all_to_all(local_peak[0], "blk", split_axis=0, concat_axis=0, tiled=True),
        lax.all_to_all(local_sum[0], "blk", split_axis=0, concat_axis=0, tiled=True),
    )
    cache_part = (
        moved_out.reshape(block_count, rows_dev, -1),
        moved_peak.reshape(block_count, rows_dev, -1),
        moved_sum.reshape(block_count, rows_dev, -1),
    )
    attention = merge_parts(cache_part, draft_part, HEAD_SIZE)
    every_row = lax.all_gather(attention, "blk", axis=0, tiled=True)
    projected = lax.psum_scatter(
        jnp.dot(every_row, out_weight, preferred_element_type=jnp.float32),
        "kv",
        scatter_dimension=0,
        tiled=True,
    ).astype(jnp.bfloat16)
    positions_here = my_block * block_len + jnp.arange(block_len, dtype=jnp.int32)
    offset = positions_here[None, :] - lengths[:, None]
    written = (offset >= 0) & (offset < accepted_count[:, None])
    slot_match = offset[:, :, None] == jnp.arange(ACC, dtype=jnp.int32)[None, None, :]
    node_ids = jnp.sum(jnp.where(slot_match, accepted_nodes[:, None, :], 0), axis=-1)
    new_cache_keys = place_rows(
        gathered_keys.reshape(requests, TREE_TOKENS, cache_width),
        node_ids,
        written,
        cached_key_vectors,
    )
    new_cache_values = place_rows(
        gathered_values.reshape(requests, TREE_TOKENS, cache_width),
        node_ids,
        written,
        cached_value_vectors,
    )
    return (projected, new_cache_keys, new_cache_values)


LOG2E = 1.4426950408889634
MESH_ID = pl.DeviceIdType.MESH
ABSENT = -1e20
PARTS = 2


def fused_kernel(
    z_count,
    kv_count,
    len_hbm,
    count_hbm,
    nodes_hbm,
    parents_hbm,
    q_hbm,
    dk_hbm,
    dv_hbm,
    key_hbm,
    value_hbm,
    weight_hbm,
    out_ref,
    new_key_hbm,
    new_value_hbm,
    len_ref,
    count_ref,
    nodes_ref,
    parents_ref,
    gq,
    tree,
    picked,
    keys,
    values,
    weight,
    own_o,
    own_st,
    xs_o,
    xs_st,
    xr_o,
    xr_st,
    zs_o,
    zs_st,
    zr_o,
    zr_st,
    ag,
    rs_send,
    rs_recv,
    local_sem,
    gz_send,
    gz_recv,
    gx_send,
    gx_recv,
    t_send,
    t_recv,
    p_send,
    p_recv,
    x_send,
    x_recv,
    z_send,
    z_recv,
    az_send,
    az_recv,
    ax_send,
    ax_recv,
    r_send,
    r_recv,
):
    kv = lax.axis_index("kv")
    blk = lax.axis_index("blk")
    z = blk // 2
    x = blk % 2
    other = 1 - x
    partner = (kv, z * 2 + other)
    rows, width_q = q_hbm.shape
    width_kv = dk_hbm.shape[1]
    groups = width_kv // HEAD_SIZE
    heads = width_q // width_kv
    cols = rows * heads
    requests, block_len, _ = keys.shape
    scale = LOG2E / math.sqrt(HEAD_SIZE)

    def z_at(step):
        return lax.rem(z + step, z_count)

    def z_back(step):
        return lax.rem(z + z_count - step, z_count)

    load_keys = pltpu.make_async_copy(key_hbm, keys, local_sem.at[0])
    load_values = pltpu.make_async_copy(value_hbm, values, local_sem.at[1])
    load_weight = pltpu.make_async_copy(weight_hbm, weight, local_sem.at[2])
    first_loads = [
        pltpu.make_async_copy(src, dst, local_sem.at[5 + i])
        for i, (src, dst) in enumerate(
            (
                (q_hbm, gq.at[blk]),
                (dk_hbm, tree.at[0, x]),
                (dv_hbm, tree.at[1, x]),
                (parents_hbm, parents_ref),
                (nodes_hbm, nodes_ref),
                (len_hbm, len_ref),
                (count_hbm, count_ref),
            )
        )
    ]
    for load in first_loads:
        load.start()
    load_keys.start()
    load_values.start()
    load_weight.start()

    barrier = pltpu.get_barrier_semaphore()
    pl.semaphore_signal(barrier, inc=1, device_id=partner, device_id_type=MESH_ID)
    for step in range(1, z_count):
        pl.semaphore_signal(
            barrier, inc=1, device_id=(kv, z_at(step) * 2 + x), device_id_type=MESH_ID
        )
    for step in range(1, kv_count):
        pl.semaphore_signal(
            barrier, inc=1, device_id=(lax.rem(kv + step, kv_count), blk), device_id_type=MESH_ID
        )
    pl.semaphore_wait(barrier, z_count + kv_count - 1)

    def remote(src, dst, send, recv, device):
        return pltpu.make_async_remote_copy(
            src_ref=src,
            dst_ref=dst,
            send_sem=send,
            recv_sem=recv,
            device_id=device,
            device_id_type=MESH_ID,
        )

    part_rows = rows // PARTS

    def piece(buf, slot, part):
        return buf.at[slot, pl.ds(part * part_rows, part_rows)]

    def gather_start(buf, zs, zr, xs, xr):
        for part in range(PARTS):
            here = piece(buf, blk, part)
            remote(here, here, xs.at[0, part], xr.at[0, part], partner).start()
            for step in range(1, z_count):
                device = (kv, z_at(step) * 2 + x)
                remote(here, here, zs.at[step, part], zr.at[step, part], device).start()

    def gather_forward(buf, part, zs, zr, xs, xr):
        for step in range(1, z_count):
            here = piece(buf, z_back(step) * 2 + x, part)
            remote(here, here, zs.at[step, part], zr.at[step, part], partner).wait_recv()
            remote(here, here, xs.at[step, part], xr.at[step, part], partner).start()

    def gather_wait(buf, step, xs, xr):
        for part in range(PARTS):
            here = piece(buf, z_back(step) * 2 + other, part)
            remote(here, here, xs.at[step, part], xr.at[step, part], partner).wait_recv()

    def gather_drain(buf, zs, zr, xs, xr):
        for part in range(PARTS):
            here = piece(buf, blk, part)
            for step in range(z_count):
                remote(here, here, xs.at[step, part], xr.at[step, part], partner).wait_send()
                if step:
                    remote(here, here, zs.at[step, part], zr.at[step, part], partner).wait_send()

    def tree_copy(which):
        own = tree.at[which, x]
        return remote(own, own, t_send.at[which], t_recv.at[which], partner)

    def picked_copy(step):
        own = picked.at[z]
        return remote(own, own, p_send.at[step], p_recv.at[step], (kv, z_at(step) * 2 + x))

    for load in first_loads[:3]:
        load.wait()
    gather_start(gq, gz_send, gz_recv, gx_send, gx_recv)
    for which in range(2):
        tree_copy(which).start()
    for load in first_loads[3:]:
        load.wait()

    node_row = lax.broadcasted_iota(jnp.int32, (TREE_TOKENS, TREE_TOKENS), 0)
    node_col = lax.broadcasted_iota(jnp.int32, (TREE_TOKENS, TREE_TOKENS), 1)
    parent_row = parents_ref[pl.ds(z, 1), :]
    reach = jnp.where(
        (node_row == node_col) | ((parent_row == node_row) & (node_col >= 1)), 1.0, 0.0
    )
    for _ in range((TREE_TOKENS - 1).bit_length()):
        half = reach.astype(jnp.bfloat16)
        reach = jnp.minimum(reach + jnp.dot(half, half, preferred_element_type=jnp.float32), 1.0)
    pick_row = lax.broadcasted_iota(jnp.int32, (TREE_TOKENS, cols), 0)
    pick_col = lax.broadcasted_iota(jnp.int32, (TREE_TOKENS, cols), 1)
    pick = jnp.where(pick_row == x * rows + lax.rem(pick_col, rows), 1.0, 0.0)
    usable = (
        jnp.dot(
            reach.astype(jnp.bfloat16),
            pick.astype(jnp.bfloat16),
            preferred_element_type=jnp.float32,
        )
        > 0.5
    )

    def stacked(slot, group):
        first = group * heads * HEAD_SIZE
        return [
            gq[slot, :, first + h * HEAD_SIZE : first + (h + 1) * HEAD_SIZE] for h in range(heads)
        ]

    def softmax_part(key_rows, value_rows, query_rows, mask):
        scores = (
            lax.dot_general(
                key_rows, query_rows, (((1,), (1,)), ((), ())), preferred_element_type=jnp.float32
            )
            * scale
        )
        scores = jnp.where(mask, scores, -1e30)
        peak = jnp.maximum(jnp.max(scores, axis=0, keepdims=True), ABSENT)
        w = jnp.exp2(scores - peak)
        total = jnp.sum(w, axis=0, keepdims=True)
        out = lax.dot_general(
            value_rows,
            w.astype(jnp.bfloat16),
            (((0,), (0,)), ((), ())),
            preferred_element_type=jnp.float32,
        )
        return out, peak, total

    position = lax.broadcasted_iota(jnp.int32, (block_len, 2 * cols), 0) + blk * block_len

    def cache_step(step):
        request = z_back(step)
        mask = position < len_ref[request]
        for g in range(groups):
            lanes = slice(g * HEAD_SIZE, (g + 1) * HEAD_SIZE)
            query_rows = jnp.concatenate(
                stacked(request * 2 + x, g) + stacked(request * 2 + other, g), axis=0
            )
            out, peak, total = softmax_part(
                keys[request, :, lanes], values[request, :, lanes], query_rows, mask
            )
            own_o[step, g] = out[:, :cols]
            xs_o[step, g] = out[:, cols:].astype(jnp.bfloat16)
            for k, stat in enumerate((peak, total, peak, total)):
                own_st[step, 4 * g + k : 4 * g + k + 1, :] = stat[:, :cols]
                xs_st[step, 4 * g + k : 4 * g + k + 1, :] = stat[:, cols:]
        for copy in x_copies(step):
            copy.start()

    def x_copies(step):
        return (
            remote(xs_o.at[step], xr_o.at[step], x_send.at[step, 0], x_recv.at[step, 0], partner),
            remote(
                xs_st.at[step], xr_st.at[step], x_send.at[step, 1], x_recv.at[step, 1], partner
            ),
        )

    def z_copies(step):
        device = (kv, z_back(step) * 2 + x)
        return (
            remote(zs_o.at[step], zr_o.at[step], z_send.at[step, 0], z_recv.at[step, 0], device),
            remote(zs_st.at[step], zr_st.at[step], z_send.at[step, 1], z_recv.at[step, 1], device),
        )

    def combine(parts):
        peak = parts[0][1]
        for part in parts[1:]:
            peak = jnp.maximum(peak, part[1])
        out = total = None
        for part_out, part_peak, part_total in parts:
            factor = jnp.exp2(part_peak - peak)
            out = part_out * factor if out is None else out + part_out * factor
            total = part_total * factor if total is None else total + part_total * factor
        return out, peak, total

    def merge_step(step):
        for copy in x_copies(step):
            copy.wait_recv()
        for g in range(groups):
            out, peak, total = combine(
                [
                    (own_o[step, g], own_st[step, 4 * g : 4 * g + 1, :], own_st[step, 4 * g + 1 : 4 * g + 2, :]),
                    (
                        xr_o[step, g].astype(jnp.float32),
                        xr_st[step, 4 * g : 4 * g + 1, :],
                        xr_st[step, 4 * g + 1 : 4 * g + 2, :],
                    ),
                ]
            )
            if step == 0:
                own_o[0, g] = out
                own_st[0, 4 * g : 4 * g + 1, :] = peak
                own_st[0, 4 * g + 1 : 4 * g + 2, :] = total
            else:
                zs_o[step, g] = out.astype(jnp.bfloat16)
                for k, stat in enumerate((peak, total, peak, total)):
                    zs_st[step, 4 * g + k : 4 * g + k + 1, :] = stat
        if step:
            for copy in z_copies(step):
                copy.start()

    load_keys.wait()
    load_values.wait()
    for which in range(2):
        tree_copy(which).wait_recv()
    slot_row = lax.broadcasted_iota(jnp.int32, (ACC, TREE_TOKENS), 0)
    slot_col = lax.broadcasted_iota(jnp.int32, (ACC, TREE_TOKENS), 1)
    node = jnp.zeros((ACC, TREE_TOKENS), jnp.int32)
    for k in range(ACC):
        node = jnp.where(slot_row == k, nodes_ref[z, k], node)
    one_hot = jnp.where(node == slot_col, 1.0, 0.0).astype(jnp.bfloat16)
    picked[z] = jnp.concatenate(
        [
            jnp.dot(
                one_hot,
                tree[which].reshape(TREE_TOKENS, width_kv),
                preferred_element_type=jnp.float32,
            )
            for which in range(2)
        ],
        axis=0,
    ).astype(jnp.bfloat16)
    for step in range(1, z_count):
        picked_copy(step).start()
    draft_parts = []
    for g in range(groups):
        lanes = slice(g * HEAD_SIZE, (g + 1) * HEAD_SIZE)
        tree_k = tree[0, :, :, lanes].reshape(TREE_TOKENS, HEAD_SIZE)
        tree_v = tree[1, :, :, lanes].reshape(TREE_TOKENS, HEAD_SIZE)
        query_rows = jnp.concatenate(stacked(blk, g), axis=0)
        draft_parts.append(softmax_part(tree_k, tree_v, query_rows, usable))
    gather_wait(gq, 0, gx_send, gx_recv)
    for part in range(PARTS):
        gather_forward(gq, part, gz_send, gz_recv, gx_send, gx_recv)
    order = list(range(1, z_count)) + [0]
    previous = None
    for step in order:
        if step:
            gather_wait(gq, step, gx_send, gx_recv)
        cache_step(step)
        if previous is not None:
            merge_step(previous)
        previous = step
    merge_step(previous)

    for step in range(1, z_count):
        picked_copy(step).wait_recv()
    update_row = lax.broadcasted_iota(jnp.int32, (block_len, 2 * ACC), 0) + blk * block_len
    update_col = lax.broadcasted_iota(jnp.int32, (block_len, 2 * ACC), 1)
    update_wide = lax.broadcasted_iota(jnp.int32, (block_len, width_kv), 0) + blk * block_len
    for r in range(requests):
        wide = update_wide - len_ref[r]
        written = (wide >= 0) & (wide < count_ref[r])
        for which, cache in enumerate((keys, values)):
            offset = update_row - len_ref[r]
            one_hot = jnp.where(
                (offset + which * ACC == update_col) & (offset >= 0) & (offset < ACC), 1.0, 0.0
            )
            placed = jnp.dot(
                one_hot.astype(jnp.bfloat16), picked[r], preferred_element_type=jnp.float32
            )
            cache[r] = jnp.where(written, placed, cache[r].astype(jnp.float32)).astype(
                jnp.bfloat16
            )
    store_keys = pltpu.make_async_copy(keys, new_key_hbm, local_sem.at[3])
    store_values = pltpu.make_async_copy(values, new_value_hbm, local_sem.at[4])
    store_keys.start()
    store_values.start()

    for step in range(1, z_count):
        for copy in z_copies(step):
            copy.wait_recv()
    for g in range(groups):
        low, high = 4 * g, 4 * g + 1
        parts = [draft_parts[g], (own_o[0, g], own_st[0, low : low + 1, :], own_st[0, high : high + 1, :])]
        for step in range(1, z_count):
            parts.append(
                (
                    zr_o[step, g].astype(jnp.float32),
                    zr_st[step, low : low + 1, :],
                    zr_st[step, high : high + 1, :],
                )
            )
        out, _, total = combine(parts)
        turned = (out / total).T.astype(jnp.bfloat16)
        for h in range(heads):
            first = (g * heads + h) * HEAD_SIZE
            ag[blk, :, first : first + HEAD_SIZE] = turned[h * rows : (h + 1) * rows, :]

    gather_start(ag, az_send, az_recv, ax_send, ax_recv)
    load_weight.wait()

    def kv_copy(row_block, source):
        return remote(
            rs_send.at[row_block],
            rs_recv.at[source],
            r_send.at[row_block],
            r_recv.at[source],
            (row_block, blk),
        )

    def project(step):
        row_block = z_back(step)
        lhs = ag[pl.ds(row_block * 2, 2)].reshape(2 * rows, width_q)
        part = jnp.dot(lhs, weight[...], preferred_element_type=jnp.float32)

        @pl.when(row_block == kv)
        def _():
            out_ref[...] = part

        @pl.when(row_block != kv)
        def _():
            rs_send[row_block] = part.astype(jnp.bfloat16)
            kv_copy(row_block, kv).start()

    gather_wait(ag, 0, ax_send, ax_recv)
    project(0)
    for part in range(PARTS):
        gather_forward(ag, part, az_send, az_recv, ax_send, ax_recv)
    for step in range(1, z_count):
        gather_wait(ag, step, ax_send, ax_recv)
        project(step)

    gather_drain(gq, gz_send, gz_recv, gx_send, gx_recv)
    gather_drain(ag, az_send, az_recv, ax_send, ax_recv)
    for step in range(z_count):
        for copy in x_copies(step):
            copy.wait_send()
        if step:
            for copy in z_copies(step):
                copy.wait_send()
    for which in range(2):
        tree_copy(which).wait_send()
    for step in range(1, z_count):
        picked_copy(step).wait_send()
    store_keys.wait()
    store_values.wait()
    for step in range(1, kv_count):
        peer = lax.rem(kv + step, kv_count)
        copy = kv_copy(peer, peer)
        copy.wait_recv()
        out_ref[...] += rs_recv[peer].astype(jnp.float32)
        copy.wait_send()


def fused(
    queries,
    draft_token_keys,
    draft_token_values,
    cached_key_vectors,
    cached_value_vectors,
    out_weight,
    lengths,
    parents,
    accepted_nodes,
    accepted_count,
):
    blk_count = lax.axis_size("blk")
    kv_count = lax.axis_size("kv")
    z_count = blk_count // 2
    rows, width_q = queries.shape
    width_kv = draft_token_keys.shape[1]
    groups = width_kv // HEAD_SIZE
    cols = rows * (width_q // width_kv)
    out_cols = out_weight.shape[1]
    out_rows = rows * blk_count // kv_count
    bf16, f32 = jnp.bfloat16, jnp.float32
    outs = pltpu.VMEM((z_count, groups, HEAD_SIZE, cols), bf16)
    stats = pltpu.VMEM((z_count, 4 * groups, cols), f32)
    vmem = pl.BlockSpec(memory_space=pltpu.VMEM)
    hbm = pl.BlockSpec(memory_space=pltpu.HBM)
    dma = pltpu.SemaphoreType.DMA
    projected, new_keys, new_values = pl.pallas_call(
        functools.partial(fused_kernel, z_count, kv_count),
        out_shape=(
            jax.ShapeDtypeStruct((out_rows, out_cols), f32),
            jax.ShapeDtypeStruct(cached_key_vectors.shape, bf16),
            jax.ShapeDtypeStruct(cached_value_vectors.shape, bf16),
        ),
        in_specs=[hbm] * 10,
        out_specs=(vmem, hbm, hbm),
        scratch_shapes=[
            pltpu.SMEM(lengths.shape, jnp.int32),
            pltpu.SMEM(accepted_count.shape, jnp.int32),
            pltpu.SMEM(accepted_nodes.shape, jnp.int32),
            pltpu.VMEM(parents.shape, jnp.int32),
            pltpu.VMEM((blk_count, rows, width_q), bf16),
            pltpu.VMEM((2, 2, rows, width_kv), bf16),
            pltpu.VMEM((z_count, 2 * ACC, width_kv), bf16),
            pltpu.VMEM(cached_key_vectors.shape, bf16),
            pltpu.VMEM(cached_value_vectors.shape, bf16),
            pltpu.VMEM(out_weight.shape, bf16),
            pltpu.VMEM((z_count, groups, HEAD_SIZE, cols), f32),
            stats,
            outs,
            stats,
            outs,
            stats,
            outs,
            stats,
            outs,
            stats,
            pltpu.VMEM((blk_count, rows, width_q), bf16),
            pltpu.VMEM((kv_count, out_rows, out_cols), bf16),
            pltpu.VMEM((kv_count, out_rows, out_cols), bf16),
            dma((12,)),
        ]
        + [dma((z_count, PARTS))] * 4
        + [dma((2,))] * 2
        + [dma((z_count,))] * 2
        + [dma((z_count, 2))] * 4
        + [dma((z_count, PARTS))] * 4
        + [dma((kv_count,))] * 2,
        compiler_params=pltpu.CompilerParams(
            collective_id=0, has_side_effects=True, vmem_limit_bytes=63 * 1024 * 1024
        ),
        cost_estimate=pl.CostEstimate(
            flops=4 * 10**9, bytes_accessed=9 * 10**6, transcendentals=2 * 10**6
        ),
    )(
        lengths,
        accepted_count,
        accepted_nodes,
        parents,
        queries,
        draft_token_keys,
        draft_token_values,
        cached_key_vectors,
        cached_value_vectors,
        out_weight,
    )
    return (projected.astype(bf16), new_keys, new_values)


def solution(mesh):
    kv_count, blk_count = mesh.shape["kv"], mesh.shape["blk"]
    paired = kv_count * 2 == blk_count and kv_count <= 4
    return jax.shard_map(
        fused if paired else on_device,
        mesh=mesh,
        in_specs=(
            P("blk", "kv"),
            P("blk", "kv"),
            P("blk", "kv"),
            P(None, "blk", "kv"),
            P(None, "blk", "kv"),
            P("kv", "blk"),
            P(),
            P(),
            P(),
            P(),
        ),
        out_specs=(P("kv", "blk"), P(None, "blk", "kv"), P(None, "blk", "kv")),
        check_vma=False,
    )
```

```python
import functools
import math

import jax
import jax.numpy as jnp
from jax import lax
from jax.experimental import pallas as pl
from jax.experimental.pallas import tpu as pltpu
from jax.sharding import PartitionSpec as P

HEAD_SIZE = 128
TREE_TOKENS = 64
ACC = 8


NEG_FLOOR = -1e30


def ancestors(parent_rows):
    node_ids = jnp.arange(TREE_TOKENS, dtype=jnp.int32)
    parent_link = (
        (parent_rows[:, :, None] == node_ids[None, None, :]) & (node_ids[None, :, None] >= 1)
    ).astype(jnp.float32)
    reachable = jnp.eye(TREE_TOKENS, dtype=jnp.float32)[None] + parent_link
    for doubling in range((TREE_TOKENS - 1).bit_length()):
        reachable = jnp.minimum(
            reachable
            + jnp.einsum("rij,rjk->rik", reachable, reachable, precision=lax.Precision.HIGHEST),
            1.0,
        )
    return reachable


def partial_softmax(query_vectors, key_rows, value_rows, usable, score_scale):
    scores = (
        jnp.einsum(
            "rtkgh,rbpkh->brkgtp", query_vectors, key_rows, preferred_element_type=jnp.float32
        )
        * score_scale
    )
    scores = jnp.where(usable, scores, NEG_FLOOR)
    peak_score = jnp.max(scores, axis=-1)
    weights = jnp.where(usable, jnp.exp(scores - peak_score[..., None]), 0.0)
    weight_sum = jnp.sum(weights, axis=-1)
    weighted = jnp.einsum(
        "brkgtp,rbpkh->brtkgh",
        weights.astype(jnp.bfloat16),
        value_rows,
        preferred_element_type=jnp.float32,
    )
    block_count, req_count, kv_count, query_group_width, row_count = peak_score.shape
    weighted = weighted.reshape(
        block_count, req_count * row_count, kv_count * query_group_width * value_rows.shape[-1]
    )
    peak_score = peak_score.transpose(0, 1, 4, 2, 3).reshape(
        block_count, req_count * row_count, kv_count * query_group_width
    )
    weight_sum = weight_sum.transpose(0, 1, 4, 2, 3).reshape(
        block_count, req_count * row_count, kv_count * query_group_width
    )
    return (weighted, peak_score, weight_sum)


def merge_parts(cache_part, draft_part, head_dim):
    cache_out, cache_peak, cache_sum = cache_part
    draft_out, draft_peak, draft_sum = draft_part
    cache_out = cache_out.astype(jnp.float32)
    overall = jnp.maximum(jnp.max(cache_peak, axis=0), draft_peak[0])
    cache_factor = jnp.exp(cache_peak - overall[None])
    draft_factor = jnp.exp(draft_peak[0] - overall)
    denominator = jnp.sum(cache_factor * cache_sum, axis=0) + draft_factor * draft_sum[0]
    block_count, row_count, head_count = cache_peak.shape
    numerator = jnp.sum(
        cache_factor[..., None] * cache_out.reshape(block_count, row_count, head_count, head_dim),
        axis=0,
    )
    numerator = numerator + draft_factor[..., None] * draft_out[0].reshape(
        row_count, head_count, head_dim
    )
    return (
        (numerator / denominator[..., None])
        .reshape(row_count, head_count * head_dim)
        .astype(jnp.bfloat16)
    )


def place_rows(sources, slot_index, written, cache_rows):
    slot_ids = jnp.arange(sources.shape[1], dtype=jnp.int32)
    selector = ((slot_index[:, :, None] == slot_ids[None, None, :]) & written[:, :, None]).astype(
        jnp.bfloat16
    )
    placed = jnp.einsum(
        "rps,rsc->rpc", selector, sources, preferred_element_type=jnp.float32
    ).astype(jnp.bfloat16)
    return jnp.where(written[:, :, None], placed, cache_rows)


def on_device(
    queries,
    draft_token_keys,
    draft_token_values,
    cached_key_vectors,
    cached_value_vectors,
    out_weight,
    lengths,
    parents,
    accepted_nodes,
    accepted_count,
):
    block_count = lax.axis_size("blk")
    my_block = lax.axis_index("blk")
    rows_dev, width_q = queries.shape
    requests = lengths.shape[0]
    cache_width = cached_key_vectors.shape[2]
    kv_local = cache_width // HEAD_SIZE
    query_group_width = width_q // (kv_local * HEAD_SIZE)
    block_len = cached_key_vectors.shape[1]
    score_scale = 1.0 / math.sqrt(HEAD_SIZE)
    leading_row = my_block * rows_dev
    my_request = leading_row // TREE_TOKENS
    node_start = leading_row - my_request * TREE_TOKENS
    local_queries = queries.reshape(1, rows_dev, kv_local, query_group_width, HEAD_SIZE)
    gathered_keys, gathered_values = (
        lax.all_gather(draft_token_keys, "blk", axis=0, tiled=True),
        lax.all_gather(draft_token_values, "blk", axis=0, tiled=True),
    )
    tree_keys = lax.dynamic_slice_in_dim(
        gathered_keys, my_request * TREE_TOKENS, TREE_TOKENS, 0
    ).reshape(1, 1, TREE_TOKENS, kv_local, HEAD_SIZE)
    tree_values = lax.dynamic_slice_in_dim(
        gathered_values, my_request * TREE_TOKENS, TREE_TOKENS, 0
    ).reshape(1, 1, TREE_TOKENS, kv_local, HEAD_SIZE)
    reachable = ancestors(lax.dynamic_slice_in_dim(parents, my_request, 1, 0))
    own_reach = lax.dynamic_slice_in_dim(reachable, node_start, rows_dev, 1)
    draft_usable = (own_reach > 0.5)[None, :, None, None, :, :]
    draft_part = partial_softmax(local_queries, tree_keys, tree_values, draft_usable, score_scale)
    every_query = lax.all_gather(queries, "blk", axis=0, tiled=True)
    all_queries = every_query.reshape(requests, TREE_TOKENS, kv_local, query_group_width, HEAD_SIZE)
    positions = my_block * block_len + jnp.arange(block_len, dtype=jnp.int32)
    usable = (positions[None, :] < lengths[:, None])[None, :, None, None, None, :]
    local_out, local_peak, local_sum = partial_softmax(
        all_queries,
        cached_key_vectors.reshape(requests, 1, block_len, kv_local, HEAD_SIZE),
        cached_value_vectors.reshape(requests, 1, block_len, kv_local, HEAD_SIZE),
        usable,
        score_scale,
    )
    moved_out = lax.all_to_all(
        local_out[0].astype(jnp.bfloat16), "blk", split_axis=0, concat_axis=0, tiled=True
    )
    moved_peak, moved_sum = (
        lax.all_to_all(local_peak[0], "blk", split_axis=0, concat_axis=0, tiled=True),
        lax.all_to_all(local_sum[0], "blk", split_axis=0, concat_axis=0, tiled=True),
    )
    cache_part = (
        moved_out.reshape(block_count, rows_dev, -1),
        moved_peak.reshape(block_count, rows_dev, -1),
        moved_sum.reshape(block_count, rows_dev, -1),
    )
    attention = merge_parts(cache_part, draft_part, HEAD_SIZE)
    every_row = lax.all_gather(attention, "blk", axis=0, tiled=True)
    projected = lax.psum_scatter(
        jnp.dot(every_row, out_weight, preferred_element_type=jnp.float32),
        "kv",
        scatter_dimension=0,
        tiled=True,
    ).astype(jnp.bfloat16)
    positions_here = my_block * block_len + jnp.arange(block_len, dtype=jnp.int32)
    offset = positions_here[None, :] - lengths[:, None]
    written = (offset >= 0) & (offset < accepted_count[:, None])
    slot_match = offset[:, :, None] == jnp.arange(ACC, dtype=jnp.int32)[None, None, :]
    node_ids = jnp.sum(jnp.where(slot_match, accepted_nodes[:, None, :], 0), axis=-1)
    new_cache_keys = place_rows(
        gathered_keys.reshape(requests, TREE_TOKENS, cache_width),
        node_ids,
        written,
        cached_key_vectors,
    )
    new_cache_values = place_rows(
        gathered_values.reshape(requests, TREE_TOKENS, cache_width),
        node_ids,
        written,
        cached_value_vectors,
    )
    return (projected, new_cache_keys, new_cache_values)


LOG2E = 1.4426950408889634
MESH_ID = pl.DeviceIdType.MESH
ABSENT = -1e20
PARTS = 2


def fused_kernel(
    z_count,
    kv_count,
    len_hbm,
    count_hbm,
    nodes_hbm,
    parents_hbm,
    q_hbm,
    dk_hbm,
    dv_hbm,
    key_hbm,
    value_hbm,
    weight_hbm,
    out_ref,
    new_key_hbm,
    new_value_hbm,
    len_ref,
    count_ref,
    nodes_ref,
    parents_ref,
    gq,
    tree,
    picked,
    keys,
    values,
    weight,
    own_o,
    own_st,
    xs_o,
    xs_st,
    xr_o,
    xr_st,
    zs_o,
    zs_st,
    zr_o,
    zr_st,
    ag,
    rs_send,
    rs_recv,
    local_sem,
    gz_send,
    gz_recv,
    gx_send,
    gx_recv,
    t_send,
    t_recv,
    p_send,
    p_recv,
    x_send,
    x_recv,
    z_send,
    z_recv,
    az_send,
    az_recv,
    ax_send,
    ax_recv,
    r_send,
    r_recv,
):
    kv = lax.axis_index("kv")
    blk = lax.axis_index("blk")
    z = blk // 2
    x = blk % 2
    other = 1 - x
    partner = (kv, z * 2 + other)
    rows, width_q = q_hbm.shape
    width_kv = dk_hbm.shape[1]
    groups = width_kv // HEAD_SIZE
    heads = width_q // width_kv
    cols = rows * heads
    requests, block_len, _ = keys.shape
    scale = LOG2E / math.sqrt(HEAD_SIZE)

    def z_at(step):
        return lax.rem(z + step, z_count)

    def z_back(step):
        return lax.rem(z + z_count - step, z_count)

    load_keys = pltpu.make_async_copy(key_hbm, keys, local_sem.at[0])
    load_values = pltpu.make_async_copy(value_hbm, values, local_sem.at[1])
    load_weight = pltpu.make_async_copy(weight_hbm, weight, local_sem.at[2])
    first_loads = [
        pltpu.make_async_copy(src, dst, local_sem.at[5 + i])
        for i, (src, dst) in enumerate(
            (
                (q_hbm, gq.at[blk]),
                (dk_hbm, tree.at[0, x]),
                (dv_hbm, tree.at[1, x]),
                (parents_hbm, parents_ref),
                (nodes_hbm, nodes_ref),
                (len_hbm, len_ref),
                (count_hbm, count_ref),
            )
        )
    ]
    for load in first_loads:
        load.start()
    load_keys.start()
    load_values.start()
    load_weight.start()

    barrier = pltpu.get_barrier_semaphore()
    pl.semaphore_signal(barrier, inc=1, device_id=partner, device_id_type=MESH_ID)
    for step in range(1, z_count):
        pl.semaphore_signal(
            barrier, inc=1, device_id=(kv, z_at(step) * 2 + x), device_id_type=MESH_ID
        )
    for step in range(1, kv_count):
        pl.semaphore_signal(
            barrier, inc=1, device_id=(lax.rem(kv + step, kv_count), blk), device_id_type=MESH_ID
        )
    pl.semaphore_wait(barrier, z_count + kv_count - 1)

    def remote(src, dst, send, recv, device):
        return pltpu.make_async_remote_copy(
            src_ref=src,
            dst_ref=dst,
            send_sem=send,
            recv_sem=recv,
            device_id=device,
            device_id_type=MESH_ID,
        )

    part_rows = rows // PARTS

    def piece(buf, slot, part):
        return buf.at[slot, pl.ds(part * part_rows, part_rows)]

    def gather_start(buf, zs, zr, xs, xr):
        for part in range(PARTS):
            here = piece(buf, blk, part)
            remote(here, here, xs.at[0, part], xr.at[0, part], partner).start()
            for step in range(1, z_count):
                device = (kv, z_at(step) * 2 + x)
                remote(here, here, zs.at[step, part], zr.at[step, part], device).start()

    def gather_forward(buf, part, zs, zr, xs, xr):
        for step in range(1, z_count):
            here = piece(buf, z_back(step) * 2 + x, part)
            remote(here, here, zs.at[step, part], zr.at[step, part], partner).wait_recv()
            remote(here, here, xs.at[step, part], xr.at[step, part], partner).start()

    def gather_wait(buf, step, xs, xr):
        for part in range(PARTS):
            here = piece(buf, z_back(step) * 2 + other, part)
            remote(here, here, xs.at[step, part], xr.at[step, part], partner).wait_recv()

    def gather_drain(buf, zs, zr, xs, xr):
        for part in range(PARTS):
            here = piece(buf, blk, part)
            for step in range(z_count):
                remote(here, here, xs.at[step, part], xr.at[step, part], partner).wait_send()
                if step:
                    remote(here, here, zs.at[step, part], zr.at[step, part], partner).wait_send()

    def tree_copy(which):
        own = tree.at[which, x]
        return remote(own, own, t_send.at[which], t_recv.at[which], partner)

    def picked_copy(step):
        own = picked.at[z]
        return remote(own, own, p_send.at[step], p_recv.at[step], (kv, z_at(step) * 2 + x))

    for load in first_loads[:3]:
        load.wait()
    gather_start(gq, gz_send, gz_recv, gx_send, gx_recv)
    for which in range(2):
        tree_copy(which).start()
    for load in first_loads[3:]:
        load.wait()

    node_row = lax.broadcasted_iota(jnp.int32, (TREE_TOKENS, TREE_TOKENS), 0)
    node_col = lax.broadcasted_iota(jnp.int32, (TREE_TOKENS, TREE_TOKENS), 1)
    parent_row = parents_ref[pl.ds(z, 1), :]
    reach = jnp.where(
        (node_row == node_col) | ((parent_row == node_row) & (node_col >= 1)), 1.0, 0.0
    )
    for _ in range((TREE_TOKENS - 1).bit_length()):
        half = reach.astype(jnp.bfloat16)
        reach = jnp.minimum(reach + jnp.dot(half, half, preferred_element_type=jnp.float32), 1.0)
    pick_row = lax.broadcasted_iota(jnp.int32, (TREE_TOKENS, cols), 0)
    pick_col = lax.broadcasted_iota(jnp.int32, (TREE_TOKENS, cols), 1)
    pick = jnp.where(pick_row == x * rows + lax.rem(pick_col, rows), 1.0, 0.0)
    usable = (
        jnp.dot(
            reach.astype(jnp.bfloat16),
            pick.astype(jnp.bfloat16),
            preferred_element_type=jnp.float32,
        )
        > 0.5
    )

    def stacked(slot, group):
        first = group * heads * HEAD_SIZE
        return [
            gq[slot, :, first + h * HEAD_SIZE : first + (h + 1) * HEAD_SIZE] for h in range(heads)
        ]

    def softmax_part(key_rows, value_rows, query_rows, mask):
        scores = (
            lax.dot_general(
                key_rows, query_rows, (((1,), (1,)), ((), ())), preferred_element_type=jnp.float32
            )
            * scale
        )
        scores = jnp.where(mask, scores, -1e30)
        peak = jnp.maximum(jnp.max(scores, axis=0, keepdims=True), ABSENT)
        w = jnp.exp2(scores - peak)
        total = jnp.sum(w, axis=0, keepdims=True)
        out = lax.dot_general(
            value_rows,
            w.astype(jnp.bfloat16),
            (((0,), (0,)), ((), ())),
            preferred_element_type=jnp.float32,
        )
        return out, peak, total

    position = lax.broadcasted_iota(jnp.int32, (block_len, 2 * cols), 0) + blk * block_len

    def cache_step(step):
        request = z_back(step)
        mask = position < len_ref[request]
        for g in range(groups):
            lanes = slice(g * HEAD_SIZE, (g + 1) * HEAD_SIZE)
            query_rows = jnp.concatenate(
                stacked(request * 2 + x, g) + stacked(request * 2 + other, g), axis=0
            )
            out, peak, total = softmax_part(
                keys[request, :, lanes], values[request, :, lanes], query_rows, mask
            )
            own_o[step, g] = out[:, :cols]
            xs_o[step, g] = out[:, cols:].astype(jnp.bfloat16)
            for k, stat in enumerate((peak, total, peak, total)):
                own_st[step, 4 * g + k : 4 * g + k + 1, :] = stat[:, :cols]
                xs_st[step, 4 * g + k : 4 * g + k + 1, :] = stat[:, cols:]
        for copy in x_copies(step):
            copy.start()

    def x_copies(step):
        return (
            remote(xs_o.at[step], xr_o.at[step], x_send.at[step, 0], x_recv.at[step, 0], partner),
            remote(
                xs_st.at[step], xr_st.at[step], x_send.at[step, 1], x_recv.at[step, 1], partner
            ),
        )

    def z_copies(step):
        device = (kv, z_back(step) * 2 + x)
        return (
            remote(zs_o.at[step], zr_o.at[step], z_send.at[step, 0], z_recv.at[step, 0], device),
            remote(zs_st.at[step], zr_st.at[step], z_send.at[step, 1], z_recv.at[step, 1], device),
        )

    def combine(parts):
        peak = parts[0][1]
        for part in parts[1:]:
            peak = jnp.maximum(peak, part[1])
        out = total = None
        for part_out, part_peak, part_total in parts:
            factor = jnp.exp2(part_peak - peak)
            out = part_out * factor if out is None else out + part_out * factor
            total = part_total * factor if total is None else total + part_total * factor
        return out, peak, total

    def merge_step(step):
        for copy in x_copies(step):
            copy.wait_recv()
        for g in range(groups):
            out, peak, total = combine(
                [
                    (own_o[step, g], own_st[step, 4 * g : 4 * g + 1, :], own_st[step, 4 * g + 1 : 4 * g + 2, :]),
                    (
                        xr_o[step, g].astype(jnp.float32),
                        xr_st[step, 4 * g : 4 * g + 1, :],
                        xr_st[step, 4 * g + 1 : 4 * g + 2, :],
                    ),
                ]
            )
            if step == 0:
                own_o[0, g] = out
                own_st[0, 4 * g : 4 * g + 1, :] = peak
                own_st[0, 4 * g + 1 : 4 * g + 2, :] = total
            else:
                zs_o[step, g] = out.astype(jnp.bfloat16)
                for k, stat in enumerate((peak, total, peak, total)):
                    zs_st[step, 4 * g + k : 4 * g + k + 1, :] = stat
        if step:
            for copy in z_copies(step):
                copy.start()

    load_keys.wait()
    load_values.wait()
    gather_wait(gq, 0, gx_send, gx_recv)
    cache_step(0)
    for which in range(2):
        tree_copy(which).wait_recv()
    slot_row = lax.broadcasted_iota(jnp.int32, (ACC, TREE_TOKENS), 0)
    slot_col = lax.broadcasted_iota(jnp.int32, (ACC, TREE_TOKENS), 1)
    node = jnp.zeros((ACC, TREE_TOKENS), jnp.int32)
    for k in range(ACC):
        node = jnp.where(slot_row == k, nodes_ref[z, k], node)
    one_hot = jnp.where(node == slot_col, 1.0, 0.0).astype(jnp.bfloat16)
    picked[z] = jnp.concatenate(
        [
            jnp.dot(
                one_hot,
                tree[which].reshape(TREE_TOKENS, width_kv),
                preferred_element_type=jnp.float32,
            )
            for which in range(2)
        ],
        axis=0,
    ).astype(jnp.bfloat16)
    for step in range(1, z_count):
        picked_copy(step).start()
    draft_parts = []
    for g in range(groups):
        lanes = slice(g * HEAD_SIZE, (g + 1) * HEAD_SIZE)
        tree_k = tree[0, :, :, lanes].reshape(TREE_TOKENS, HEAD_SIZE)
        tree_v = tree[1, :, :, lanes].reshape(TREE_TOKENS, HEAD_SIZE)
        query_rows = jnp.concatenate(stacked(blk, g), axis=0)
        draft_parts.append(softmax_part(tree_k, tree_v, query_rows, usable))
    for part in range(PARTS):
        gather_forward(gq, part, gz_send, gz_recv, gx_send, gx_recv)
    merge_step(0)
    for step in range(1, z_count):
        gather_wait(gq, step, gx_send, gx_recv)
        cache_step(step)
        if step > 1:
            merge_step(step - 1)
    merge_step(z_count - 1)

    for step in range(1, z_count):
        picked_copy(step).wait_recv()
    update_row = lax.broadcasted_iota(jnp.int32, (block_len, 2 * ACC), 0) + blk * block_len
    update_col = lax.broadcasted_iota(jnp.int32, (block_len, 2 * ACC), 1)
    update_wide = lax.broadcasted_iota(jnp.int32, (block_len, width_kv), 0) + blk * block_len
    for r in range(requests):
        wide = update_wide - len_ref[r]
        written = (wide >= 0) & (wide < count_ref[r])
        for which, cache in enumerate((keys, values)):
            offset = update_row - len_ref[r]
            one_hot = jnp.where(
                (offset + which * ACC == update_col) & (offset >= 0) & (offset < ACC), 1.0, 0.0
            )
            placed = jnp.dot(
                one_hot.astype(jnp.bfloat16), picked[r], preferred_element_type=jnp.float32
            )
            cache[r] = jnp.where(written, placed, cache[r].astype(jnp.float32)).astype(
                jnp.bfloat16
            )
    store_keys = pltpu.make_async_copy(keys, new_key_hbm, local_sem.at[3])
    store_values = pltpu.make_async_copy(values, new_value_hbm, local_sem.at[4])
    store_keys.start()
    store_values.start()

    for step in range(1, z_count):
        for copy in z_copies(step):
            copy.wait_recv()
    for g in range(groups):
        low, high = 4 * g, 4 * g + 1
        parts = [draft_parts[g], (own_o[0, g], own_st[0, low : low + 1, :], own_st[0, high : high + 1, :])]
        for step in range(1, z_count):
            parts.append(
                (
                    zr_o[step, g].astype(jnp.float32),
                    zr_st[step, low : low + 1, :],
                    zr_st[step, high : high + 1, :],
                )
            )
        out, _, total = combine(parts)
        turned = (out / total).T.astype(jnp.bfloat16)
        for h in range(heads):
            first = (g * heads + h) * HEAD_SIZE
            ag[blk, :, first : first + HEAD_SIZE] = turned[h * rows : (h + 1) * rows, :]

    gather_start(ag, az_send, az_recv, ax_send, ax_recv)
    load_weight.wait()

    def kv_copy(row_block, source):
        return remote(
            rs_send.at[row_block],
            rs_recv.at[source],
            r_send.at[row_block],
            r_recv.at[source],
            (row_block, blk),
        )

    def project(step):
        row_block = z_back(step)
        lhs = ag[pl.ds(row_block * 2, 2)].reshape(2 * rows, width_q)
        part = jnp.dot(lhs, weight[...], preferred_element_type=jnp.float32)

        @pl.when(row_block == kv)
        def _():
            out_ref[...] = part

        @pl.when(row_block != kv)
        def _():
            rs_send[row_block] = part.astype(jnp.bfloat16)
            kv_copy(row_block, kv).start()

    gather_wait(ag, 0, ax_send, ax_recv)
    project(0)
    for part in range(PARTS):
        gather_forward(ag, part, az_send, az_recv, ax_send, ax_recv)
    for step in range(1, z_count):
        gather_wait(ag, step, ax_send, ax_recv)
        project(step)

    gather_drain(gq, gz_send, gz_recv, gx_send, gx_recv)
    gather_drain(ag, az_send, az_recv, ax_send, ax_recv)
    for step in range(z_count):
        for copy in x_copies(step):
            copy.wait_send()
        if step:
            for copy in z_copies(step):
                copy.wait_send()
    for which in range(2):
        tree_copy(which).wait_send()
    for step in range(1, z_count):
        picked_copy(step).wait_send()
    store_keys.wait()
    store_values.wait()
    for step in range(1, kv_count):
        peer = lax.rem(kv + step, kv_count)
        copy = kv_copy(peer, peer)
        copy.wait_recv()
        out_ref[...] += rs_recv[peer].astype(jnp.float32)
        copy.wait_send()


def fused(
    queries,
    draft_token_keys,
    draft_token_values,
    cached_key_vectors,
    cached_value_vectors,
    out_weight,
    lengths,
    parents,
    accepted_nodes,
    accepted_count,
):
    blk_count = lax.axis_size("blk")
    kv_count = lax.axis_size("kv")
    z_count = blk_count // 2
    rows, width_q = queries.shape
    width_kv = draft_token_keys.shape[1]
    groups = width_kv // HEAD_SIZE
    cols = rows * (width_q // width_kv)
    out_cols = out_weight.shape[1]
    out_rows = rows * blk_count // kv_count
    bf16, f32 = jnp.bfloat16, jnp.float32
    outs = pltpu.VMEM((z_count, groups, HEAD_SIZE, cols), bf16)
    stats = pltpu.VMEM((z_count, 4 * groups, cols), f32)
    vmem = pl.BlockSpec(memory_space=pltpu.VMEM)
    hbm = pl.BlockSpec(memory_space=pltpu.HBM)
    dma = pltpu.SemaphoreType.DMA
    projected, new_keys, new_values = pl.pallas_call(
        functools.partial(fused_kernel, z_count, kv_count),
        out_shape=(
            jax.ShapeDtypeStruct((out_rows, out_cols), f32),
            jax.ShapeDtypeStruct(cached_key_vectors.shape, bf16),
            jax.ShapeDtypeStruct(cached_value_vectors.shape, bf16),
        ),
        in_specs=[hbm] * 10,
        out_specs=(vmem, hbm, hbm),
        scratch_shapes=[
            pltpu.SMEM(lengths.shape, jnp.int32),
            pltpu.SMEM(accepted_count.shape, jnp.int32),
            pltpu.SMEM(accepted_nodes.shape, jnp.int32),
            pltpu.VMEM(parents.shape, jnp.int32),
            pltpu.VMEM((blk_count, rows, width_q), bf16),
            pltpu.VMEM((2, 2, rows, width_kv), bf16),
            pltpu.VMEM((z_count, 2 * ACC, width_kv), bf16),
            pltpu.VMEM(cached_key_vectors.shape, bf16),
            pltpu.VMEM(cached_value_vectors.shape, bf16),
            pltpu.VMEM(out_weight.shape, bf16),
            pltpu.VMEM((z_count, groups, HEAD_SIZE, cols), f32),
            stats,
            outs,
            stats,
            outs,
            stats,
            outs,
            stats,
            outs,
            stats,
            pltpu.VMEM((blk_count, rows, width_q), bf16),
            pltpu.VMEM((kv_count, out_rows, out_cols), bf16),
            pltpu.VMEM((kv_count, out_rows, out_cols), bf16),
            dma((12,)),
        ]
        + [dma((z_count, PARTS))] * 4
        + [dma((2,))] * 2
        + [dma((z_count,))] * 2
        + [dma((z_count, 2))] * 4
        + [dma((z_count, PARTS))] * 4
        + [dma((kv_count,))] * 2,
        compiler_params=pltpu.CompilerParams(
            collective_id=0, has_side_effects=True, vmem_limit_bytes=63 * 1024 * 1024
        ),
        cost_estimate=pl.CostEstimate(
            flops=4 * 10**9, bytes_accessed=9 * 10**6, transcendentals=2 * 10**6
        ),
    )(
        lengths,
        accepted_count,
        accepted_nodes,
        parents,
        queries,
        draft_token_keys,
        draft_token_values,
        cached_key_vectors,
        cached_value_vectors,
        out_weight,
    )
    return (projected.astype(bf16), new_keys, new_values)


def solution(mesh):
    kv_count, blk_count = mesh.shape["kv"], mesh.shape["blk"]
    paired = kv_count * 2 == blk_count and kv_count <= 4
    return jax.shard_map(
        fused if paired else on_device,
        mesh=mesh,
        in_specs=(
            P("blk", "kv"),
            P("blk", "kv"),
            P("blk", "kv"),
            P(None, "blk", "kv"),
            P(None, "blk", "kv"),
            P("kv", "blk"),
            P(),
            P(),
            P(),
            P(),
        ),
        out_specs=(P("kv", "blk"), P(None, "blk", "kv"), P(None, "blk", "kv")),
        check_vma=False,
    )
```
